32 devices in a mesh: dp: 8 (over y, x, core), seq: 4 (over z).
Axes of the slice: x: 2, y: 2, z: 4, core: 2. Of those that a mesh axis runs over, the one named last changes fastest.
Arguments:
- image_tokens: bfloat16 [16, 1024, 1152], P('dp', 'seq'), may hold values from -6 to 6
- cotangent: bfloat16 [16, 1024, 1152], P('dp', 'seq'), may hold values from -6 to 6
- targets: bfloat16 [16, 1024, 768], P('dp', 'seq'), may hold values from -8 to 8
- bucket: int32 [16], P('dp'), may hold values from 0 to 999, as said below
- labels: int32 [16], P('dp'), may hold values from 0 to 999
- time_table: float32 [1000, 1152], replicated, may hold values from -6 to 6
- class_table: float32 [1000, 1152], replicated, may hold values from -6 to 6
- ada_weight: float32 [1152, 6912], P('dp'), may hold values from -0.1875 to 0.1875
- ada_bias: float32 [6912], P('dp'), may hold values from -4 to 4
- qkv_weight: float32 [1152, 3456], P('dp'), may hold values from -0.25 to 0.25
- qkv_bias: float32 [3456], P('dp'), may hold values from -4 to 4
- out_weight: float32 [1152, 1152], P('dp'), may hold values from -2 to 2
- out_bias: float32 [1152], P('dp'), may hold values from -4 to 4
- up_weight: float32 [1152, 4608], P('dp'), may hold values from -0.1875 to 0.1875
- up_bias: float32 [4608], P('dp'), may hold values from -4 to 4
- down_weight: float32 [4608, 1152], P('dp'), may hold values from -0.09375 to 0.09375
- down_bias: float32 [1152], P('dp'), may hold values from -4 to 4
- tap_first: float32 [1152, 2048], P('dp'), may hold values from -0.1875 to 0.1875
- tap_first_bias: float32 [2048], P('dp'), may hold values from -4 to 4
- tap_second: float32 [2048, 2048], P('dp'), may hold values from -0.125 to 0.125
- tap_second_bias: float32 [2048], P('dp'), may hold values from -4 to 4
- tap_third: float32 [2048, 768], P('dp'), may hold values from -0.125 to 0.125
- tap_third_bias: float32 [768], P('dp'), may hold values from -6 to 6
Outputs:
- block_output: bfloat16 [16, 1024, 1152], P('dp', 'seq')
- input_grad: float32 [16, 1024, 1152], P('dp', 'seq')
- align_loss: float32 [], replicated
- time_table_grad: float32 [1000, 1152], replicated
- class_table_grad: float32 [1000, 1152], replicated
- ada_weight_grad: float32 [1152, 6912], P('dp')
- ada_bias_grad: float32 [6912], P('dp')
- qkv_weight_grad: float32 [1152, 3456], P('dp')
- qkv_bias_grad: float32 [3456], P('dp')
- out_weight_grad: float32 [1152, 1152], P('dp')
- out_bias_grad: float32 [1152], P('dp')
- up_weight_grad: float32 [1152, 4608], P('dp')
- up_bias_grad: float32 [4608], P('dp')
- down_weight_grad: float32 [4608, 1152], P('dp')
- down_bias_grad: float32 [1152], P('dp')
- tap_first_grad: float32 [1152, 2048], P('dp')
- tap_first_bias_grad: float32 [2048], P('dp')
- tap_second_grad: float32 [2048, 2048], P('dp')
- tap_second_bias_grad: float32 [2048], P('dp')
- tap_third_grad: float32 [2048, 768], P('dp')
- tap_third_bias_grad: float32 [768], P('dp')
The draws below stay inside these ranges and needn't reach their ends.
Inputs may be any that keep to these rules, and one draw needn't show every extreme that they name: `bucket`: bell-shaped over the buckets, most images near the middle one; one image at each end of the range.
All inputs are finite; a program needn't handle non-finite values.
Results may differ from the reference program's by a relative error of at most 0.024.
The reference program's roundings to bfloat16 on the way count: a program that leaves them out, or rounds other values in their place, can miss the bound.
Values may be sent and summed in bfloat16 or wider, within the bound.
No kernel may reach another device: no remote copies, remote signals or barrier semaphores. Data moves between devices by JAX's collectives and lax.ppermute only.
A program may use at most 448 MiB of HBM per device.

```python
import math
import jax
import jax.numpy as jnp
from jax import lax

D = 1152
HEADS = 16
HEAD_DIM = 72
FF = 4608
CLASSES = 1000
BUCKETS = 1000
TAP_HIDDEN = 2048
TAP_OUT = 768
PATCHES = 1024
IMAGES = 16
TOTAL = 16384


def shared_feature(key):
    return jnp.clip(jax.random.normal(key, (TAP_OUT,), jnp.float32), -4.0, 4.0)


def draw_bucket(key, part):
    key = jax.random.fold_in(key, 7)
    draws = jax.random.randint(key, (3, IMAGES), 0, BUCKETS, dtype=jnp.int32)
    middle = (jnp.sum(draws, axis=0) // 3).astype(jnp.int32)
    order = jax.random.permutation(jax.random.fold_in(key, 1), IMAGES).astype(jnp.int32)
    places = jnp.arange(IMAGES, dtype=jnp.int32)
    middle = jnp.where(places == order[0], jnp.int32(BUCKETS - 1), middle)
    middle = jnp.where(places == order[1], jnp.int32(0), middle)
    return middle.astype(jnp.int32)


def draw_targets(key, part):
    common = shared_feature(key)
    key = jax.random.fold_in(key, 11)
    noise = jnp.clip(jax.random.normal(key, (IMAGES, PATCHES, TAP_OUT), jnp.float32), -5.0, 5.0)
    return (common[None, None, :] + 0.6 * noise).astype(jnp.bfloat16)


def draw_tap_third_bias(key, part):
    common = shared_feature(key)
    key = jax.random.fold_in(key, 13)
    noise = jnp.clip(jax.random.normal(key, (TAP_OUT,), jnp.float32), -5.0, 5.0)
    return (0.8 * common + 0.3 * noise).astype(jnp.float32)


def plant(entries, key, low, top_value):
    dims = entries.shape
    place = [jax.random.randint(jax.random.fold_in(key, axis), (), 0, dims[axis]) for axis in range(len(dims))]
    entries = entries.at[tuple(place)].set(low)
    longest = dims.index(max(dims))
    place[longest] = (place[longest] + 1) % dims[longest]
    return entries.at[tuple(place)].set(top_value)


def levels(key, extent, cuts, low, top_value):
    gain, own = 1.0, jax.random.fold_in(key, 6)
    for dim, shards_of in cuts:
        steps = jnp.exp(jax.random.uniform(jax.random.fold_in(own, dim), (shards_of,), jnp.float32, low / len(cuts), top_value / len(cuts)))
        gain = gain * jnp.repeat(steps, extent[dim] // shards_of).reshape([-1 if axis == dim else 1 for axis in range(len(extent))])
    return gain


def scatter_about(stream_key, dims, deviation, bound, shards=(), held_as=jnp.bfloat16):
    array = deviation * jax.random.normal(stream_key, dims, jnp.float32)
    if shards:
        array = array * levels(stream_key, dims, shards, -0.22, 0.18)
    return jnp.clip(array, -bound, bound).astype(held_as)


def setup_inputs(seed: int = 0) -> dict:
    arg_keys = jax.random.split(jax.random.key(seed), 24)
    return {
        "image_tokens": scatter_about(arg_keys[0], (IMAGES, PATCHES, D), 1.0, 6.0, ((0, 8), (1, 4))),
        "cotangent": scatter_about(arg_keys[1], (IMAGES, PATCHES, D), 1.0, 6.0, ((0, 8), (1, 4))),
        "targets": draw_targets(jax.random.fold_in(arg_keys[23], 71), 0),
        "bucket": draw_bucket(jax.random.fold_in(arg_keys[23], 71), 0),
        "labels": plant(jax.random.randint(arg_keys[4], (IMAGES,), 0, CLASSES), jax.random.fold_in(arg_keys[4], 1), 0, CLASSES - 1).astype(jnp.int32),
        "time_table": scatter_about(arg_keys[5], (BUCKETS, D), 1.0, 6.0, (), jnp.float32),
        "class_table": scatter_about(arg_keys[6], (CLASSES, D), 1.0, 6.0, (), jnp.float32),
        "ada_weight": scatter_about(arg_keys[7], (D, 6 * D), D ** -0.5, 0.1875, ((0, 8),), jnp.float32),
        "ada_bias": scatter_about(arg_keys[8], (6 * D,), 0.3, 4.0, ((0, 8),), jnp.float32),
        "qkv_weight": scatter_about(arg_keys[9], (D, 3 * D), (D // 2) ** -0.5, 0.25, ((0, 8),), jnp.float32),
        "qkv_bias": scatter_about(arg_keys[10], (3 * D,), 0.3, 4.0, ((0, 8),), jnp.float32),
        "out_weight": scatter_about(arg_keys[11], (D, D), (max(1, D // 128)) ** -0.5, 2.0, ((0, 8),), jnp.float32),
        "out_bias": scatter_about(arg_keys[12], (D,), 0.3, 4.0, ((0, 8),), jnp.float32),
        "up_weight": scatter_about(arg_keys[13], (D, FF), D ** -0.5, 0.1875, ((0, 8),), jnp.float32),
        "up_bias": scatter_about(arg_keys[14], (FF,), 0.3, 4.0, ((0, 8),), jnp.float32),
        "down_weight": scatter_about(arg_keys[15], (FF, D), FF ** -0.5, 0.09375, ((0, 8),), jnp.float32),
        "down_bias": scatter_about(arg_keys[16], (D,), 0.3, 4.0, ((0, 8),), jnp.float32),
        "tap_first": scatter_about(arg_keys[17], (D, TAP_HIDDEN), D ** -0.5, 0.1875, ((0, 8),), jnp.float32),
        "tap_first_bias": scatter_about(arg_keys[18], (TAP_HIDDEN,), 0.3, 4.0, ((0, 8),), jnp.float32),
        "tap_second": scatter_about(arg_keys[19], (TAP_HIDDEN, TAP_HIDDEN), TAP_HIDDEN ** -0.5, 0.125, ((0, 8),), jnp.float32),
        "tap_second_bias": scatter_about(arg_keys[20], (TAP_HIDDEN,), 0.3, 4.0, ((0, 8),), jnp.float32),
        "tap_third": scatter_about(arg_keys[21], (TAP_HIDDEN, TAP_OUT), TAP_HIDDEN ** -0.5, 0.125, ((0, 8),), jnp.float32),
        "tap_third_bias": draw_tap_third_bias(jax.random.fold_in(arg_keys[23], 71), 0),
    }


@jax.custom_vjp
def low(v):
    return lax.optimization_barrier(v.astype(jnp.bfloat16)).astype(jnp.float32)

@jax.custom_vjp
def low_back(v):
    return v

def low_keep(v):
    return (low(v), None)

def low_pass(kept, grad):
    return (grad,)

def back_keep(v):
    return (v, None)

def back_low(kept, grad):
    return (low(grad),)
low.defvjp(low_keep, low_pass)
low_back.defvjp(back_keep, back_low)
EPS_NORM = 1e-06
HIGH = lax.Precision.HIGHEST

def layer_norm(values):
    centre = values - lax.optimization_barrier(jnp.mean(values, axis=-1, keepdims=True))
    spread = lax.optimization_barrier(jnp.mean(centre * centre, axis=-1, keepdims=True))
    return centre * lax.rsqrt(spread + EPS_NORM)

def dense(values, weight, bias):
    return jnp.einsum('...i,ij->...j', values, weight, precision=HIGH) + bias

def cosine(latent, target):
    inner = lax.optimization_barrier(jnp.sum(latent * target, axis=-1))
    return inner * lax.rsqrt(lax.optimization_barrier(jnp.sum(latent * latent, axis=-1)) + EPS_NORM) * lax.rsqrt(lax.optimization_barrier(jnp.sum(target * target, axis=-1)) + EPS_NORM)

def group_forward(weights, tokens, target, condition):
    ada_weight, ada_bias, qkv_weight, qkv_bias, out_weight, out_bias, up_weight, up_bias, down_weight, down_bias, tap_first, tap_first_bias, tap_second, tap_second_bias, tap_third, tap_third_bias = weights
    images = tokens.shape[0]
    modulation = dense(low(jax.nn.silu(condition)), ada_weight, ada_bias)
    shift_one, scale_one, gate_one, shift_two, scale_two, gate_two = jnp.split(modulation[:, None, :], 6, axis=-1)
    hidden_one = low(layer_norm(tokens) * (1.0 + scale_one) + shift_one)
    qkv = low(low_back(dense(hidden_one, qkv_weight, qkv_bias)))
    queries, keys_all, values_all = jnp.split(qkv, 3, axis=-1)
    queries = queries.reshape(images, PATCHES, HEADS, HEAD_DIM)
    keys_all = keys_all.reshape(images, PATCHES, HEADS, HEAD_DIM)
    values_all = values_all.reshape(images, PATCHES, HEADS, HEAD_DIM)
    raw = jnp.einsum('bqhd,bkhd->bhqk', queries, keys_all, precision=HIGH)
    scores = low_back(raw * (1.0 / math.sqrt(HEAD_DIM)))
    probs = low(jax.nn.softmax(scores, axis=-1))
    context = jnp.einsum('bhqk,bkhd->bqhd', probs, values_all, precision=HIGH).reshape(images, PATCHES, D)
    context = low(low_back(context))
    attended = low_back(dense(context, out_weight, out_bias))
    mixed = tokens + gate_one * attended
    hidden_two = low(layer_norm(mixed) * (1.0 + scale_two) + shift_two)
    upper = low_back(dense(hidden_two, up_weight, up_bias))
    act = low(jax.nn.gelu(upper, approximate=True))
    feed = low_back(dense(act, down_weight, down_bias))
    output = mixed + gate_two * feed
    first_pre = low_back(dense(low(output), tap_first, tap_first_bias))
    first = low(jax.nn.silu(first_pre))
    second_pre = low_back(dense(first, tap_second, tap_second_bias))
    second = low(jax.nn.silu(second_pre))
    latent = low_back(dense(second, tap_third, tap_third_bias))
    return (output, jnp.sum(cosine(latent, target)))

def reference(image_tokens, cotangent, targets, bucket, labels, time_table, class_table, ada_weight, ada_bias, qkv_weight, qkv_bias, out_weight, out_bias, up_weight, up_bias, down_weight, down_bias, tap_first, tap_first_bias, tap_second, tap_second_bias, tap_third, tap_third_bias):
    group = math.gcd(IMAGES, max(1, 4096 // PATCHES))
    blocks = IMAGES // group
    tokens32 = image_tokens.astype(jnp.float32)
    target32 = targets.astype(jnp.float32).reshape(blocks, group, PATCHES, TAP_OUT)
    weights = (ada_weight, ada_bias, qkv_weight, qkv_bias, out_weight, out_bias, up_weight, up_bias, down_weight, down_bias, tap_first, tap_first_bias, tap_second, tap_second_bias, tap_third, tap_third_bias)

    def forward(tokens_in, tables, params):
        time_tab, class_tab = tables
        condition = time_tab[bucket] + class_tab[labels]
        lowered = tuple((low(item) for item in params))

        def step(items):
            return group_forward(lowered, items[0], items[1], items[2])
        outputs, sums = lax.map(jax.checkpoint(step), (tokens_in.reshape(blocks, group, PATCHES, D), target32, condition.reshape(blocks, group, D)))
        loss = -0.5 * jnp.sum(sums) / TOTAL
        return (outputs.reshape(IMAGES, PATCHES, D), loss)
    (output, loss), pullback = jax.vjp(forward, tokens32, (time_table, class_table), weights)
    token_grad, table_grads, grads = pullback((cotangent.astype(jnp.float32), jnp.ones((), jnp.float32) * TOTAL))
    return (output.astype(jnp.bfloat16), token_grad, loss, table_grads[0], table_grads[1], grads[0], grads[1], grads[2], grads[3], grads[4], grads[5], grads[6], grads[7], grads[8], grads[9], grads[10], grads[11], grads[12], grads[13], grads[14], grads[15])
```

```python
import functools
import math

import jax
import jax.numpy as jnp
from jax import lax
from jax.experimental import pallas as pl
from jax.experimental.pallas import tpu as pltpu
from jax.sharding import PartitionSpec as P

HEADS = 16
HEAD_DIM = 72
EPS_NORM = 1e-06
HIGH = lax.Precision.HIGHEST
HALF = jnp.bfloat16
WIDE = jnp.float32
VMEM_BYTES = 56 * 1024 * 1024
GELU_A = math.sqrt(2.0 / math.pi)
GELU_B = 0.044715
SCALE = 1
MARK = (8, 128)
DONE = {}
TAKES = {
    "qkv": 13,
    "attention": 30,
    "out": 8,
    "feed": 27,
    "tap": 16,
    "latent": 9,
    "cosine": 9,
    "tap_back": 16,
    "third_grad": 5,
    "second_grad": 8,
    "first_grad": 6,
    "feed_back": 28,
    "down_grad": 12,
    "up_grad": 12,
    "mix_back": 14,
    "out_grad": 5,
    "attention_back": 31,
    "qkv_back": 12,
    "qkv_grad": 10,
    "input_grad": 5,
    "split_qkv": 3,
    "split_rest": 3,
    "pack_near": 4,
    "pack_far": 4,
    "condition": 2,
}


def cost(microseconds):
    return pl.CostEstimate(
        flops=int(microseconds * SCALE * 1.15e9),
        bytes_accessed=int(microseconds * SCALE * 3.6e6),
        transcendentals=0,
    )


def dot(left, right):
    return jnp.dot(left, right, preferred_element_type=WIDE)


def dot_nt(left, right):
    return lax.dot_general(left, right, (((1,), (1,)), ((), ())), preferred_element_type=WIDE)


def normed(values):
    centre = values - jnp.mean(values, axis=-1, keepdims=True)
    spread = jnp.mean(centre * centre, axis=-1, keepdims=True)
    inverse = lax.rsqrt(spread + EPS_NORM)
    return centre * inverse, inverse


def normed_back(norm, inverse, grad):
    return (
        grad
        - jnp.mean(grad, axis=-1, keepdims=True)
        - norm * jnp.mean(grad * norm, axis=-1, keepdims=True)
    ) * inverse


def sigmoid(values):
    return 1.0 / (1.0 + jnp.exp(-values))


def silu_back(pre, grad):
    gate = sigmoid(pre)
    return grad * (gate * (1.0 + pre * (1.0 - gate)))


def gelu(values):
    inner = jnp.tanh(GELU_A * (values + GELU_B * (values * values * values)))
    return 0.5 * values * (1.0 + inner)


def gelu_back(values, grad):
    square = values * values
    inner = jnp.tanh(GELU_A * (values + GELU_B * (square * values)))
    slope = 0.5 * (1.0 + inner) + 0.5 * values * (1.0 - inner * inner) * (
        GELU_A * (1.0 + 3.0 * GELU_B * square)
    )
    return grad * slope


def total(values):
    return jnp.sum(values, axis=0, keepdims=True)


def spans(size, most):
    count = -(-size // most)
    while size % count or (size // count) % 128:
        count += 1
        if count > size // 128:
            return [(0, size)]
    return [(k * (size // count), size // count) for k in range(count)]


def joined(ref, index=slice(None)):
    return jnp.concatenate([ref[h] for h in range(ref.shape[0])], axis=-1)


class Weight:
    def __init__(self, me, step, arrays, how, store, sems):
        self.me, self.step, self.arrays, self.how = me, step, arrays, how
        self.store, self.sems = store, sems

    def copies(self):
        groups, by_me, height, _ = self.how
        count = 0
        for places, pieces in groups:
            for r, (number, base) in enumerate(places):
                start = pl.multiple_of((self.me ^ r) * height, height) if by_me else r * height
                for row, rows, column, columns, to_row, to_column in pieces:
                    yield pltpu.make_async_copy(
                        self.arrays[number].at[pl.ds(base + row, rows), pl.ds(column, columns)],
                        self.store.at[pl.ds(start + to_row, rows), pl.ds(to_column, columns)],
                        self.sems.at[count],
                    )
                    count += 1

    def start(self):
        @pl.when(self.step == 0)
        def _():
            for copy in self.copies():
                copy.start()

    def ready(self):
        @pl.when(self.step == 0)
        def _():
            for copy in self.copies():
                copy.wait()

        return self.store


def token_kernel(body, counts, hows, me_ref, *refs):
    n_tok, n_const, n_blocks, n_after, n_out, n_sum = counts
    refs = list(refs)
    take = lambda n: [refs.pop(0) for _ in range(n)]
    toks, consts = take(n_tok), take(n_const)
    blocks = [take(n) for n in n_blocks]
    take(n_after)
    outs, sums, (mark,) = take(n_out), take(n_sum), take(1)
    step = pl.program_id(0)

    @pl.when(step == 0)
    def _():
        mark[...] = jnp.zeros_like(mark)

    weights = [
        Weight(me_ref[0], step, group, hows[k], refs[2 * k], refs[2 * k + 1])
        for k, group in enumerate(blocks)
    ]
    for weight in weights:
        weight.start()
    if sums:

        @pl.when(step == 0)
        def _():
            for ref in sums:
                ref[...] = jnp.zeros_like(ref)

    body(toks, consts, weights, outs, sums)


def token_call(name, body, me, toks, consts, weights, outs, sums, rows, tile, after=()):
    steps = rows // tile

    def spec(shape, dim, swapped=False):
        block = tuple(tile if k == dim else s for k, s in enumerate(shape))

        def place(i, me_ref):
            at = lax.rem(i + steps // 2, steps) if swapped else i
            return tuple(at if k == dim else 0 for k in range(len(shape)))

        return pl.BlockSpec(block, place)

    def whole(shape):
        return pl.BlockSpec(shape, lambda i, me_ref: (0,) * len(shape))

    in_specs = [spec(a.shape, a.ndim - 2, swapped) for a, swapped in toks]
    in_specs += [whole(c.shape) for c in consts]
    blocks = [array for group, _ in weights for array in group]
    in_specs += [pl.BlockSpec(memory_space=pl.ANY)] * (len(blocks) + len(after))
    out_specs = [spec(shape, dim) for shape, _, dim in outs] + [whole(shape) for shape in sums]
    out_shape = [jax.ShapeDtypeStruct(shape, dtype) for shape, dtype, _ in outs]
    out_shape += [jax.ShapeDtypeStruct(shape, WIDE) for shape in sums]
    out_specs.append(whole(MARK))
    out_shape.append(jax.ShapeDtypeStruct(MARK, WIDE))
    scratch = []
    for _, (groups, _, height, columns) in weights:
        scratch += [
            pltpu.VMEM((height * len(groups[0][0]), columns), HALF),
            pltpu.SemaphoreType.DMA((sum(len(a) * len(b) for a, b in groups),)),
        ]
    counts = (len(toks), len(consts), [len(g) for g, _ in weights], len(after), len(outs), len(sums))
    *found, DONE[name] = pl.pallas_call(
        functools.partial(token_kernel, body, counts, [how for _, how in weights]),
        grid_spec=pltpu.PrefetchScalarGridSpec(
            num_scalar_prefetch=1,
            grid=(steps,),
            in_specs=in_specs,
            out_specs=out_specs,
            scratch_shapes=scratch,
        ),
        out_shape=out_shape,
        compiler_params=pltpu.CompilerParams(
            dimension_semantics=("arbitrary",), vmem_limit_bytes=VMEM_BYTES
        ),
        cost_estimate=cost(TAKES[name]),
        name=name,
    )(me, *[a for a, _ in toks], *consts, *blocks, *after)
    return found


def qkv_body(toks, consts, weights, outs, sums):
    (x,), (shift, scale, bias), (weight,) = toks, consts, weights
    hidden_t, query, key, value = outs
    norm, _ = normed(x[...].astype(WIDE))
    hidden = norm * (1.0 + scale[...]) + shift[...]
    low = hidden.astype(HALF)
    hidden_t[...] = hidden.T.astype(HALF)
    store = weight.ready()
    width = store.shape[1] // 3
    for k, out in enumerate((query, key, value)):
        part = dot(low, store[:, k * width : (k + 1) * width])
        part = (part + bias[:, k * width : (k + 1) * width]).astype(HALF)
        for h in range(out.shape[0]):
            out[h] = part[:, h * HEAD_DIM : (h + 1) * HEAD_DIM]


def attention_kernel(query, key, value, *refs):
    context, lse, mark = refs[-3:]
    mark[...] = jnp.zeros_like(mark)
    factor = 1.0 / math.sqrt(HEAD_DIM)
    keys, values = key[0], value[0]
    rows = query.shape[1]
    tile = min(rows, 256)
    for start in range(0, rows, tile):
        at = slice(start, start + tile)
        scores = dot_nt(keys, query[0, at, :]) * factor
        highest = jnp.max(scores, axis=0, keepdims=True)
        expo = jnp.exp(scores - highest)
        summed = jnp.sum(expo, axis=0, keepdims=True)
        probs = (expo / summed).astype(HALF)
        lse[0, :, at] = highest + jnp.log(summed)
        found = lax.dot_general(
            values, probs, (((0,), (0,)), ((), ())), preferred_element_type=WIDE
        )
        context[0, at, :] = found.T.astype(HALF)


def attention_call(query, key, value, after=()):
    heads, rows, _ = query.shape
    block = pl.BlockSpec((1, rows, HEAD_DIM), lambda h: (h, 0, 0))
    line = pl.BlockSpec((1, 1, rows), lambda h: (h, 0, 0))
    *found, DONE["attention"] = pl.pallas_call(
        attention_kernel,
        grid=(heads,),
        in_specs=[block] * 3 + [pl.BlockSpec(memory_space=pl.ANY)] * len(after),
        out_specs=[block, line, pl.BlockSpec(MARK, lambda h: (0, 0))],
        out_shape=[
            jax.ShapeDtypeStruct(query.shape, HALF),
            jax.ShapeDtypeStruct((heads, 1, rows), WIDE),
            jax.ShapeDtypeStruct(MARK, WIDE),
        ],
        compiler_params=pltpu.CompilerParams(
            dimension_semantics=("arbitrary",), vmem_limit_bytes=VMEM_BYTES
        ),
        cost_estimate=cost(TAKES["attention"]),
        name="attention",
    )(query, key, value, *after)
    return found


def attention_back_kernel(query, key, value, grad, lse, *refs):
    dquery, dkey, dvalue, mark, sum_key, sum_value = refs[-6:]
    mark[...] = jnp.zeros_like(mark)
    factor = 1.0 / math.sqrt(HEAD_DIM)
    keys, values = key[0], value[0]
    rows = query.shape[1]
    tile = min(rows, 256)
    for start in range(0, rows, tile):
        at = slice(start, start + tile)
        queries, grads = query[0, at, :], grad[0, at, :]
        probs = jnp.exp(dot_nt(keys, queries) * factor - lse[0, :, at])
        dprobs = dot_nt(values, grads)
        held = jnp.sum(probs * dprobs, axis=0, keepdims=True)
        dscores = (probs * (dprobs - held)).astype(HALF)
        value_part = dot(probs.astype(HALF), grads)
        key_part = dot(dscores, queries)
        if start == 0:
            sum_value[...] = value_part
            sum_key[...] = key_part
        else:
            sum_value[...] += value_part
            sum_key[...] += key_part
        found = lax.dot_general(
            keys, dscores, (((0,), (0,)), ((), ())), preferred_element_type=WIDE
        )
        dquery[0, at, :] = (found * factor).T.astype(HALF)
    dkey[0] = (sum_key[...] * factor).astype(HALF)
    dvalue[0] = sum_value[...].astype(HALF)


def attention_back_call(query, key, value, grad, lse, after=()):
    heads, rows, _ = query.shape
    block = pl.BlockSpec((1, rows, HEAD_DIM), lambda h: (h, 0, 0))
    line = pl.BlockSpec((1, 1, rows), lambda h: (h, 0, 0))
    *found, DONE["attention_back"] = pl.pallas_call(
        attention_back_kernel,
        grid=(heads,),
        in_specs=[block] * 4 + [line] + [pl.BlockSpec(memory_space=pl.ANY)] * len(after),
        out_specs=[block] * 3 + [pl.BlockSpec(MARK, lambda h: (0, 0))],
        out_shape=[jax.ShapeDtypeStruct(query.shape, HALF)] * 3
        + [jax.ShapeDtypeStruct(MARK, WIDE)],
        scratch_shapes=[pltpu.VMEM((rows, HEAD_DIM), WIDE)] * 2,
        compiler_params=pltpu.CompilerParams(
            dimension_semantics=("arbitrary",), vmem_limit_bytes=VMEM_BYTES
        ),
        cost_estimate=cost(TAKES["attention_back"]),
        name="attention_back",
    )(query, key, value, grad, lse, *after)
    return found


def out_body(toks, consts, weights, outs, sums):
    (context,), (weight,) = toks, weights
    part, low, context_t = outs
    heads = joined(context)
    context_t[...] = heads.astype(WIDE).T.astype(HALF)
    found = dot(heads, weight.ready()[...])
    part[...] = found
    low[...] = found.astype(HALF)


def feed_body(toks, consts, weights, outs, sums):
    x, part, other = toks
    gate_one, shift, scale, out_bias, up_bias = consts
    up, down = weights
    mixed, hidden_t, upper, act_t, feed, feed_low = outs
    attended = part[...] + other[...].astype(WIDE) + out_bias[...]
    mix = x[...].astype(WIDE) + gate_one[...] * attended
    mixed[...] = mix
    norm, _ = normed(mix)
    hidden = norm * (1.0 + scale[...]) + shift[...]
    low = hidden.astype(HALF)
    hidden_t[...] = hidden.T.astype(HALF)
    up_store = up.ready()
    acc = None
    for k, (start, size) in enumerate(spans(up_store.shape[1], 768)):
        at = slice(start, start + size)
        pre = dot(low, up_store[:, at]) + up_bias[:, at]
        upper[:, at] = pre
        act = gelu(pre)
        act_t[at, :] = act.T.astype(HALF)
        if k == 0:
            down_store = down.ready()
        term = dot(act.astype(HALF), down_store[at, :])
        acc = term if acc is None else acc + term
    feed[...] = acc
    feed_low[...] = acc.astype(HALF)


def tap_body(toks, consts, weights, outs, sums):
    mixed, part, other = toks
    gate_two, down_bias, first_bias = consts
    first, second = weights
    block_out, block_t, first_pre, first_t, own, sent = outs
    feed = part[...] + other[...].astype(WIDE) + down_bias[...]
    output = mixed[...] + gate_two[...] * feed
    low = output.astype(HALF)
    block_out[...] = low
    block_t[...] = output.T.astype(HALF)
    pre = dot(low, first.ready()[...]) + first_bias[...]
    first_pre[...] = pre
    act = pre * sigmoid(pre)
    first_t[...] = act.T.astype(HALF)
    act_low = act.astype(HALF)
    store = second.ready()
    half = store.shape[1] // 2
    own[...] = dot(act_low, store[:, :half])
    sent[...] = dot(act_low, store[:, half:]).astype(HALF)


def latent_body(toks, consts, weights, outs, sums):
    (part, other), (bias,), (third,) = toks, consts, weights
    second_pre, second_t, own, low = outs
    pre = part[...] + other[...].astype(WIDE) + bias[...]
    second_pre[...] = pre
    act = pre * sigmoid(pre)
    second_t[...] = act.T.astype(HALF)
    found = dot(act.astype(HALF), third.ready()[...])
    own[...] = found
    low[...] = found.astype(HALF)


def cosine_body(toks, consts, weights, outs, sums):
    part, other, targets, second_pre = toks
    (bias,), (third,) = consts, weights
    dlatent, dsecond = outs
    cos_sum, third_bias_sum, second_bias_sum = sums
    latent = part[...] + other[...].astype(WIDE) + bias[...]
    target = targets[...].astype(WIDE)
    inner = jnp.sum(latent * target, axis=-1, keepdims=True)
    length = jnp.sum(latent * latent, axis=-1, keepdims=True) + EPS_NORM
    inverse = lax.rsqrt(length)
    inverse_target = lax.rsqrt(jnp.sum(target * target, axis=-1, keepdims=True) + EPS_NORM)
    cos = inner * inverse * inverse_target
    cos_sum[...] += jnp.broadcast_to(total(cos), cos_sum.shape)
    low = (-0.5 * (target * (inverse * inverse_target) - latent * (cos / length))).astype(HALF)
    dlatent[...] = low
    third_bias_sum[...] += total(low.astype(WIDE))
    pre_grad = silu_back(second_pre[...], dot_nt(low, third.ready()[...])).astype(HALF)
    dsecond[...] = pre_grad
    second_bias_sum[...] += total(pre_grad.astype(WIDE))


def tap_back_body(toks, consts, weights, outs, sums):
    own, other, first_pre = toks
    second, first = weights
    dfirst, part, low = outs
    (bias_sum,) = sums
    grads = jnp.concatenate([own[...], other[...]], axis=-1)
    pre_grad = silu_back(first_pre[...], dot_nt(grads, second.ready()[...])).astype(HALF)
    dfirst[...] = pre_grad
    bias_sum[...] += total(pre_grad.astype(WIDE))
    found = dot_nt(pre_grad, first.ready()[...])
    part[...] = found
    low[...] = found.astype(HALF)


def feed_back_body(toks, consts, weights, outs, sums):
    cotangent, part, other, feed_part, feed_other, upper = toks
    gate_two, down_bias = consts
    down, up = weights
    doutput, dfeed, dupper, hidden, hidden_low = outs
    gate_sum, down_bias_sum, up_bias_sum = sums
    grad = cotangent[...].astype(WIDE) + part[...] + other[...].astype(WIDE)
    doutput[...] = grad
    feed = feed_part[...] + feed_other[...].astype(WIDE) + down_bias[...]
    gate_sum[...] += total(grad * feed)
    low = (grad * gate_two[...]).astype(HALF)
    dfeed[...] = low
    down_bias_sum[...] += total(low.astype(WIDE))
    down_store = down.ready()
    acc = None
    for k, (start, size) in enumerate(spans(down_store.shape[0], 768)):
        at = slice(start, start + size)
        pre_grad = gelu_back(upper[:, at], dot_nt(low, down_store[at, :])).astype(HALF)
        dupper[:, at] = pre_grad
        up_bias_sum[:, at] += total(pre_grad.astype(WIDE))
        if k == 0:
            up_store = up.ready()
        term = dot_nt(pre_grad, up_store[:, at])
        acc = term if acc is None else acc + term
    hidden[...] = acc
    hidden_low[...] = acc.astype(HALF)


def mix_back_body(toks, consts, weights, outs, sums):
    mixed, doutput, part, other, out_part, out_other = toks
    scale, gate_one, out_bias = consts
    (weight,) = weights
    dmixed, dattended, dcontext = outs
    shift_sum, scale_sum, gate_sum, bias_sum = sums
    grad = part[...] + other[...].astype(WIDE)
    norm, inverse = normed(mixed[...])
    shift_sum[...] += total(grad)
    scale_sum[...] += total(grad * norm)
    mix_grad = doutput[...] + normed_back(norm, inverse, grad * (1.0 + scale[...]))
    dmixed[...] = mix_grad
    attended = out_part[...] + out_other[...].astype(WIDE) + out_bias[...]
    gate_sum[...] += total(mix_grad * attended)
    low = (mix_grad * gate_one[...]).astype(HALF)
    dattended[...] = low
    bias_sum[...] += total(low.astype(WIDE))
    found = dot_nt(low, weight.ready()[...]).astype(HALF)
    for h in range(dcontext.shape[0]):
        dcontext[h] = found[:, h * HEAD_DIM : (h + 1) * HEAD_DIM]


def qkv_back_body(toks, consts, weights, outs, sums):
    (weight,) = weights
    grads, part, low = outs
    (bias_sum,) = sums
    row = jnp.concatenate([joined(ref) for ref in toks], axis=-1)
    grads[...] = row
    bias_sum[...] += total(row.astype(WIDE))
    found = dot_nt(row, weight.ready()[...])
    part[...] = found
    low[...] = found.astype(HALF)


def input_body(toks, consts, weights, outs, sums):
    x, dmixed, part, other = toks
    (scale,) = consts
    (found,) = outs
    shift_sum, scale_sum = sums
    grad = part[...] + other[...].astype(WIDE)
    norm, inverse = normed(x[...].astype(WIDE))
    shift_sum[...] += total(grad)
    scale_sum[...] += total(grad * norm)
    result = dmixed[...] + normed_back(norm, inverse, grad * (1.0 + scale[...]))
    found[...] = result.astype(HALF)


def weight_grad_kernel(plan, size, sides, me_ref, left, *refs):
    count = 2 * len(plan)
    rights, (*outs, mark, hold) = refs[:sides], refs[-2 - count :]
    mark[...] = jnp.zeros_like(mark)

    def emit(found):
        hold[...] = found.astype(hold.dtype)
        for (ranks, row, rows), near, far in zip(plan, outs[::2], outs[1::2]):
            for k, r in enumerate(ranks):
                start = pl.multiple_of((me_ref[0] ^ r) * size + row, math.gcd(size, row or size))
                out = near if k < len(ranks) // 2 else far
                at = k % (len(ranks) // 2) * rows
                out[at : at + rows, :] = hold[pl.ds(start, rows), :].astype(HALF)

    if sides == 1:
        emit(dot(left[...], rights[0][...]))
        return
    is_own = pl.program_id(0) < pl.num_programs(0) // 2

    @pl.when(is_own)
    def _():
        emit(dot(left[...], rights[0][...]))

    @pl.when(jnp.logical_not(is_own))
    def _():
        half = left.shape[1] // 2
        emit(
            dot(left[:, :half], rights[1][half:, :]) + dot(left[:, half:], rights[1][:half, :])
        )


def weight_grad_call(name, me, left, rights, plan, tile, after=()):
    features, rows = left.shape
    columns = rights[0].shape[1]
    sides = len(rights)
    size = features // len(plan[0][0])
    tile = min(tile, columns)
    steps = pl.cdiv(columns, tile)
    hold = HALF if all(row % 16 == 0 and part % 16 == 0 for _, row, part in plan) else WIDE
    assert sides == 1 or columns % tile == 0
    outs = [(part * len(ranks) // 2, sides * columns) for ranks, _, part in plan for _ in range(2)]
    *found, DONE[name] = pl.pallas_call(
        functools.partial(weight_grad_kernel, plan, size, sides),
        grid_spec=pltpu.PrefetchScalarGridSpec(
            num_scalar_prefetch=1,
            grid=(sides * steps,),
            in_specs=[
                pl.BlockSpec((features, rows), lambda n, me_ref: (0, 0)),
                pl.BlockSpec((rows, tile), lambda n, me_ref: (0, jnp.minimum(n, steps - 1))),
                pl.BlockSpec((rows, tile), lambda n, me_ref: (0, jnp.maximum(n - steps, 0))),
            ][: 1 + sides]
            + [pl.BlockSpec(memory_space=pl.ANY)] * len(after),
            out_specs=[pl.BlockSpec((o[0], tile), lambda n, me_ref: (0, n)) for o in outs]
            + [pl.BlockSpec(MARK, lambda n, me_ref: (0, 0))],
            scratch_shapes=[pltpu.VMEM((features, tile), hold)],
        ),
        out_shape=[jax.ShapeDtypeStruct(o, HALF) for o in outs]
        + [jax.ShapeDtypeStruct(MARK, WIDE)],
        compiler_params=pltpu.CompilerParams(
            dimension_semantics=("arbitrary",), vmem_limit_bytes=VMEM_BYTES
        ),
        cost_estimate=cost(TAKES[name]),
        name=name,
    )(me, left, *rights, *after)
    return found


def split_kernel(plan, core_ref, *refs):
    ins, outs = refs[: len(plan)], list(refs[len(plan) :])
    for ref, (kind, groups, chips) in zip(ins, plan):
        if kind == "cast":
            outs.pop(0)[...] = ref[...].astype(HALF)
            continue
        size = ref.shape[1] // (groups * chips * 2)
        pick = lambda odd: jnp.concatenate(
            [ref[:, (2 * k + odd) * size : (2 * k + odd + 1) * size] for k in range(groups * chips)],
            axis=1,
        )
        even, odd = pick(0), pick(1)
        is_even = core_ref[0] == 0
        own = jnp.where(is_even, even, odd).astype(HALF)
        other = jnp.where(is_even, odd, even).astype(HALF)
        if kind == "split":
            outs.pop(0)[...] = own
            outs.pop(0)[...] = other
        else:
            out = outs.pop(0)
            out[:, : own.shape[1]] = own
            out[:, own.shape[1] :] = other


def split_call(name, core, weights, plan):
    outs = []
    for weight, (kind, _, _) in zip(weights, plan):
        size, columns = weight.shape
        if kind == "split":
            outs += [jax.ShapeDtypeStruct((size, columns // 2), HALF)] * 2
        else:
            outs.append(jax.ShapeDtypeStruct((size, columns), HALF))
    return pl.pallas_call(
        functools.partial(split_kernel, plan),
        in_specs=[pl.BlockSpec(memory_space=pltpu.SMEM)]
        + [pl.BlockSpec(memory_space=pltpu.VMEM)] * len(weights),
        out_specs=[pl.BlockSpec(memory_space=pltpu.VMEM)] * len(outs),
        out_shape=outs,
        compiler_params=pltpu.CompilerParams(vmem_limit_bytes=VMEM_BYTES),
        cost_estimate=cost(TAKES[name]),
        name=name,
    )(core, *weights)


def pack_kernel(width, split_count, chips, core_ref, *refs):
    *ins, out = refs
    at = 0
    for k in range(split_count):
        own, other = ins[2 * k], ins[2 * k + 1]
        rows = own.shape[0]
        is_even = core_ref[0] == 0
        for column in range(0, own.shape[1], width):
            mine, came = own[:, column : column + width], other[:, column : column + width]
            out[at : at + rows, :] = jnp.where(is_even, mine, came)
            out[at + rows : at + 2 * rows, :] = jnp.where(is_even, came, mine)
            at += 2 * rows
    for ref in ins[2 * split_count :]:
        rows, columns = ref.shape
        if chips and ref is ins[-1]:
            size = columns // (2 * chips)
            even, odd = (
                jnp.concatenate(
                    [ref[:, (2 * k + o) * size : (2 * k + o + 1) * size] for k in range(chips)],
                    axis=1,
                )
                for o in (0, 1)
            )
            is_even = core_ref[0] == 0
            whole = [jnp.where(is_even, even, odd), jnp.where(is_even, odd, even)]
            found = [v[:, c : c + width] for v in whole for c in range(0, columns // 2, width)]
        else:
            found = [ref[:, c : c + width] for c in range(0, columns, width)]
        for value in found:
            out[at : at + rows, :] = value.astype(HALF)
            at += rows


def pack_call(name, core, width, split, plain, chips=0):
    ins = [a for pair in split for a in pair] + list(plain)
    size = sum(a.size for a in ins) // width
    return pl.pallas_call(
        functools.partial(pack_kernel, width, len(split), chips),
        in_specs=[pl.BlockSpec(memory_space=pltpu.SMEM)]
        + [pl.BlockSpec(memory_space=pltpu.VMEM)] * len(ins),
        out_specs=pl.BlockSpec(memory_space=pltpu.VMEM),
        out_shape=jax.ShapeDtypeStruct((size, width), HALF),
        compiler_params=pltpu.CompilerParams(vmem_limit_bytes=VMEM_BYTES),
        cost_estimate=cost(TAKES[name]),
        name=name,
    )(core, *ins)


def condition_kernel(buckets, labels, times, classes, out, one, two, sems):
    count = out.shape[0]

    def copies(i):
        yield pltpu.make_async_copy(
            times.at[pl.ds(buckets[i], 1), :], one.at[pl.ds(i, 1), :], sems.at[0, i]
        )
        yield pltpu.make_async_copy(
            classes.at[pl.ds(labels[i], 1), :], two.at[pl.ds(i, 1), :], sems.at[1, i]
        )

    for i in range(count):
        for copy in copies(i):
            copy.start()
    for i in range(count):
        for copy in copies(i):
            copy.wait()
    out[...] = one[...] + two[...]


def condition_call(buckets, labels, times, classes):
    shape = (buckets.shape[0], times.shape[1])
    return pl.pallas_call(
        condition_kernel,
        in_specs=[pl.BlockSpec(memory_space=pltpu.SMEM)] * 2
        + [pl.BlockSpec(memory_space=pl.ANY)] * 2,
        out_specs=pl.BlockSpec(memory_space=pltpu.VMEM),
        out_shape=jax.ShapeDtypeStruct(shape, WIDE),
        scratch_shapes=[
            pltpu.VMEM(shape, WIDE),
            pltpu.VMEM(shape, WIDE),
            pltpu.SemaphoreType.DMA((2, shape[0])),
        ],
        cost_estimate=cost(TAKES["condition"]),
        name="condition",
    )(buckets, labels, times, classes)


def join_kernel(groups, chips, core_ref, own, other, out):
    size = own.shape[1] // (groups * chips)
    is_even = core_ref[0] == 0
    even = jnp.where(is_even, own[...], other[...]).astype(WIDE)
    odd = jnp.where(is_even, other[...], own[...]).astype(WIDE)
    parts = []
    for k in range(groups * chips):
        parts += [v[:, k * size : (k + 1) * size] for v in (even, odd)]
    out[...] = jnp.concatenate(parts, axis=1)


def join_call(name, core, own, other, groups, chips):
    rows, columns = own.shape
    return pl.pallas_call(
        functools.partial(join_kernel, groups, chips),
        in_specs=[pl.BlockSpec(memory_space=pltpu.SMEM)]
        + [pl.BlockSpec(memory_space=pltpu.VMEM)] * 2,
        out_specs=pl.BlockSpec(memory_space=pltpu.VMEM),
        out_shape=jax.ShapeDtypeStruct((rows, 2 * columns), WIDE),
        compiler_params=pltpu.CompilerParams(vmem_limit_bytes=VMEM_BYTES),
        cost_estimate=cost(4),
        name=name,
    )(core, own, other)


def last_kernel(value, *refs):
    refs[-1][...] = value[...]


def last_call(value, after):
    return pl.pallas_call(
        last_kernel,
        in_specs=[pl.BlockSpec(memory_space=pltpu.VMEM)]
        + [pl.BlockSpec(memory_space=pl.ANY)] * len(after),
        out_specs=pl.BlockSpec(memory_space=pltpu.VMEM),
        out_shape=jax.ShapeDtypeStruct(value.shape, value.dtype),
        cost_estimate=cost(1),
        name="last",
    )(value, *after)


def shards(
    n_dp,
    n_seq,
    image_tokens,
    cotangent,
    targets,
    bucket,
    labels,
    time_table,
    class_table,
    ada_weight,
    ada_bias,
    qkv_weight,
    qkv_bias,
    out_weight,
    out_bias,
    up_weight,
    up_bias,
    down_weight,
    down_bias,
    tap_first,
    tap_first_bias,
    tap_second,
    tap_second_bias,
    tap_third,
    tap_third_bias,
):
    images, part_rows, width = image_tokens.shape
    chips = n_dp // 2
    bits = chips.bit_length() - 1
    assert 1 << bits == chips and 2 * images == n_seq and n_seq & (n_seq - 1) == 0
    rows = 2 * images * part_rows
    place = lax.axis_index("dp")
    plane = lax.axis_index("seq")
    core, chip = place % 2, place // 2
    first_core = core == 0
    me = chip.astype(jnp.int32).reshape(1)

    def flip_core(array):
        return lax.ppermute(array, "dp", [(i, i ^ 1) for i in range(n_dp)])

    def flip_chip(array, bit):
        return lax.ppermute(array, "dp", [(i, i ^ (2 << bit)) for i in range(n_dp)])

    def flip_plane(array, bit):
        return lax.ppermute(array, "seq", [(i, i ^ (1 << bit)) for i in range(n_seq)])

    spent = []

    def later(array, *done):
        if not done:
            return array
        marks = []
        for item in done:
            item = DONE[item] if isinstance(item, str) else item
            marks.append(item)
        array, *marks = lax.optimization_barrier((array, *marks))
        spent.extend(marks)
        return array

    def pull(have, level, first):
        for r in range(chips):
            if r.bit_count() == level:
                bit = next(
                    b for b in ((first + k) % bits for k in range(bits)) if r >> b & 1
                )
                have[r] = flip_chip(have[r ^ 1 << bit], bit)

    def ranks(first):
        order = [(first + k) % bits for k in range(bits)]
        return sorted(range(chips), key=lambda r: [r >> b & 1 for b in order])

    def scatter_begin(arrays, plan, *done):
        found = []
        for k, (order, _, _) in enumerate(plan):
            first = next(f for f in range(bits) if ranks(f) == order)
            came = flip_chip(arrays[2 * k + 1], first)
            found.append(([arrays[2 * k], later(came, *done)], first))
        sent = []
        for parts, first in found:
            for step in range(1, bits):
                half = parts[0].shape[0] // 2
                far = sum(p[half:].astype(WIDE) for p in parts).astype(HALF)
                came = flip_chip(far, (first + step) % bits)
                parts = [p[:half] for p in parts] + [came]
            sent.append(parts)
        return sent, [parts[1] for parts, _ in found]

    def scatter_end(sent, *done):
        found = [
            sum(p.astype(WIDE) for p in (*parts[:-1], later(parts[-1], *done))).astype(HALF)
            for parts in sent
        ]
        return found[0] if len(found) == 1 else jnp.concatenate(found)

    def halves(size):
        if size % 32:
            return [(ranks(0), 0, size)]
        return [(ranks(0), 0, size // 2), (ranks(1 % bits), size // 2, size // 2)]

    def sum_line(array, *windows):
        extra = n_seq // 4
        for bit in range(extra.bit_length() - 1):
            array = (array.astype(WIDE) + flip_plane(array, bit).astype(WIDE)).astype(HALF)

        def move(what, pairs):
            pairs = [(a * extra + k, b * extra + k) for a, b in pairs for k in range(extra)]
            return lax.ppermute(what, "seq", pairs)

        at = plane // extra
        half = array.shape[0] // 2
        came = later(move(array, [(0, 1), (3, 2)]), *windows)
        array = (array.astype(WIDE) + came.astype(WIDE)).astype(HALF)
        low, high = array[:half], array[half:]
        came = move(jnp.where(at == 1, high, low), [(1, 2), (2, 1)])
        kept = (jnp.where(at == 1, low, high).astype(WIDE) + came.astype(WIDE)).astype(HALF)
        came = move(kept, [(1, 2), (2, 1)])
        array = jnp.where(
            at == 1, jnp.concatenate([kept, came]), jnp.concatenate([came, kept])
        )
        came = move(array, [(1, 0), (2, 3)])
        return jnp.where((at == 1) | (at == 2), array, came)

    def sum_planes(array, seen=None):
        steps = range(n_seq.bit_length() - 1)
        for bit in steps:
            half = array.shape[0] // 2
            low, high = array[:half], array[half:]
            upper = (plane >> bit & 1) == 1
            came = flip_plane(jnp.where(upper, low, high), bit)
            if seen is not None:
                seen.append(came)
            array = (jnp.where(upper, high, low).astype(WIDE) + came.astype(WIDE)).astype(HALF)
        for bit in reversed(steps):
            came = flip_plane(array, bit)
            if seen is not None:
                seen.append(came)
            upper = (plane >> bit & 1) == 1
            array = jnp.where(
                upper, jnp.concatenate([came, array]), jnp.concatenate([array, came])
            )
        return array

    def routes(turn):
        pairs = []
        for at in range(n_dp):
            for z in range(n_seq):
                k = z ^ turn
                goal = (at - at % 2 + k // images, (at % 2) * images + k % images)
                pairs.append((at * n_seq + z, goal[0] * n_seq + goal[1]))
        return pairs

    def to_chip(array, depth, *after):
        half = array.shape[1] // 2
        found = []
        for turn in range(n_seq):
            k = plane ^ turn
            piece = lax.dynamic_slice(
                array, (k % images, (k // images) * half, 0), (1, half, array.shape[2])
            )[0]
            piece = later(piece, *([found[-depth]] if len(found) >= depth else []), *after)
            found.append(lax.ppermute(piece, ("dp", "seq"), routes(turn)))
        return found

    def from_chip(array, depth, windows=((),) * 4):
        half = array.shape[0] // n_seq
        found = []
        for turn in range(n_seq):
            back = [(b, a) for a, b in routes(turn)]
            piece = array[turn * half : (turn + 1) * half]
            piece = later(piece, *([found[-depth]] if len(found) >= depth else []))
            came = lax.ppermute(piece, ("dp", "seq"), back)
            found.append(later(came, *windows[turn % len(windows)]))
        pieces = list(found)
        stacked = jnp.stack(found)
        for bit in range(n_seq.bit_length() - 1):
            pairs = stacked.reshape(-1, 2, 1 << bit, *stacked.shape[1:])
            swapped = jnp.where((plane >> bit & 1) == 1, pairs[:, ::-1], pairs)
            stacked = swapped.reshape(stacked.shape)
        parts = stacked.reshape(2, images, half, array.shape[1])
        return parts.transpose(1, 0, 2, 3).reshape(images, 2 * half, array.shape[1]), pieces

    def by_core(array, groups):
        lead = array.shape[:-1]
        cut = array.reshape(*lead, groups, chips, 2, -1)
        even = cut[..., 0, :].reshape(*lead, -1)
        odd = cut[..., 1, :].reshape(*lead, -1)
        return jnp.where(first_core, even, odd), jnp.where(first_core, odd, even)

    def from_cores(own, other, groups):
        lead = own.shape[:-1]
        even = jnp.where(first_core, own, other).reshape(*lead, groups, chips, 1, -1)
        odd = jnp.where(first_core, other, own).reshape(*lead, groups, chips, 1, -1)
        return jnp.concatenate([even, odd], axis=-2).reshape(*lead, -1)

    def in_order(own, other):
        return jnp.where(
            first_core, jnp.concatenate([own, other]), jnp.concatenate([other, own])
        )

    def spread(array, columns):
        return jnp.concatenate(
            [array[:, k : k + columns] for k in range(0, array.shape[1], columns)]
        )

    def weight_of(groups, columns, height):
        if all(v % 16 == 0 for _, pieces in groups for p in pieces for v in (p[0], p[1], p[4], height)):
            arrays, found = [], []
            for places, pieces in groups:
                numbers = []
                for array, base in places:
                    known = [k for k, seen in enumerate(arrays) if seen is array]
                    numbers.append((known[0] if known else len(arrays), base))
                    if not known:
                        arrays.append(array)
                found.append((numbers, pieces))
            return arrays, (found, True, height, columns)
        blocks = []
        for r in range(chips):
            block = jnp.zeros((height, columns), HALF)
            for places, pieces in groups:
                array, base = places[r]
                for row, rows, column, wide, to_row, to_column in pieces:
                    part = array[base + row : base + row + rows, column : column + wide]
                    block = lax.dynamic_update_slice(block, part, (to_row, to_column))
            blocks.append(block)
        stacked = jnp.take(jnp.stack(blocks), jnp.arange(chips) ^ chip, axis=0)
        stacked = stacked.reshape(-1, columns)
        size = stacked.shape[0]
        return [stacked], ([([(0, 0)], [(0, size, 0, columns, 0, 0)])], False, size, columns)

    def stacked_weight(places, at, width, columns, height):
        pieces = [
            (at + k * height, height, 0, width, 0, k * width) for k in range(columns // width)
        ]
        return weight_of([(places, pieces)], columns, height)

    biases = (
        ada_bias,
        qkv_bias,
        out_bias,
        up_bias,
        down_bias,
        tap_first_bias,
        tap_second_bias,
        tap_third_bias,
    )
    core_at = core.astype(jnp.int32).reshape(1)
    qkv_own, qkv_other = split_call("split_qkv", core_at, [qkv_weight], [("split", 3, chips)])
    qkv_have = {0: in_order(qkv_own, flip_core(qkv_other))}
    pull(qkv_have, 1, 0)
    qkv_near = [qkv_have[1 << b] for b in range(bits)]
    def pull_rest(have, first):
        for level in range(2, bits + 1):
            pull(have, level, first)
        return [have[r] for r in range(chips) if r.bit_count() > 1]

    def pull_parts(have, split):
        places, came = [[None] * chips for _ in range(2)], []
        for k in range(2):
            part = {r: have[r][:split] if k == 0 else have[r][split:] for r in have}
            came.append(pull_rest(part, 1 - k))
            for r in range(chips):
                places[k][r] = (have[r], k * split) if r in have else (part[r], 0)
        return places, came

    qkv_height, qkv_columns = qkv_have[0].shape
    (low_places, high_places), (low_last, high_last) = pull_parts(qkv_have, qkv_height // 2)
    qkv_weights = weight_of(
        [
            (places, [(0, qkv_height // 2, 0, qkv_columns, at, 0)])
            for places, at in ((low_places, 0), (high_places, qkv_height // 2))
        ],
        qkv_columns,
        qkv_height,
    )
    qkv_rest = low_last + high_last
    tokens_pieces = to_chip(image_tokens, 2, qkv_have[0])
    tokens_own = jnp.concatenate(tokens_pieces, axis=0)
    packed = jnp.concatenate(
        [b.astype(HALF).astype(WIDE) for b in biases]
        + [bucket.astype(WIDE), labels.astype(WIDE)]
    )
    everyone = jnp.pad(packed, (0, -packed.shape[0] % 128)).reshape(1, -1)
    everyone = jnp.concatenate([everyone, flip_core(everyone)])
    for bit in range(bits):
        everyone = jnp.concatenate([everyone, flip_chip(everyone, bit)])
    everyone = jnp.concatenate(
        [
            lax.dynamic_slice(everyone, (place ^ d, 0), (1, everyone.shape[1]))
            for d in range(n_dp)
        ]
    )
    full, at = [], 0
    for bias in biases:
        full.append(everyone[:, at : at + bias.shape[0]].reshape(1, -1))
        at += bias.shape[0]
    bucket_all = everyone[:, at : at + images].reshape(-1).astype(jnp.int32)
    labels_all = everyone[:, at + images : at + 2 * images].reshape(-1).astype(jnp.int32)
    ada_bias_full, qkv_bias_full, out_bias_full, up_bias_full = full[:4]
    down_bias_full, first_bias_full, second_bias_full, third_bias_full = full[4:]
    qkv_bias_own = by_core(qkv_bias_full, 3)[0]
    up_bias_own = by_core(up_bias_full, 1)[0]
    first_bias_own = by_core(first_bias_full, 1)[0]
    second_bias_own = by_core(second_bias_full, 1)[0]

    condition = condition_call(bucket_all, labels_all, time_table, class_table)
    shard = ada_weight.shape[0]
    condition_own = lax.dynamic_slice(
        condition, (0, place * shard), (condition.shape[0], shard)
    )
    cond_act, cond_back = jax.vjp(jax.nn.silu, condition_own)
    cond_low = cond_act.astype(HALF)
    cond_plane = lax.dynamic_index_in_dim(
        cond_low.reshape(chips, n_seq, shard), plane, axis=1, keepdims=False
    )
    ada_low = ada_weight.astype(HALF)
    modulation = jnp.dot(cond_plane, ada_low, preferred_element_type=WIDE)
    modulation = later(modulation, *qkv_rest)
    modulation = modulation + flip_core(modulation)
    ranked = [
        lax.dynamic_slice(modulation, (chip ^ r, 0), (1, modulation.shape[1]))
        for r in range(chips)
    ]
    for bit in reversed(range(bits)):
        half = 1 << bit
        came = flip_chip(jnp.concatenate(ranked[half : 2 * half]), bit)
        ranked = [ranked[r] + came[r : r + 1] for r in range(half)]
    modulation = ranked[0] + ada_bias_full
    shift_one, scale_one, gate_one, shift_two, scale_two, gate_two = jnp.split(
        modulation, 6, axis=-1
    )

    up_weight = later(up_weight, qkv_have[0])
    up_own, up_other, first_own, first_other = split_call(
        "split_rest",
        core_at,
        [up_weight, tap_first],
        [("split", 1, chips), ("split", 1, chips)],
    )
    same_core = [[2 * k + c for k in range(chips)] for c in range(2)]


    up_came, first_came = flip_core(up_other), flip_core(first_other)
    wide, narrow = width, math.gcd(tap_second.shape[1], tap_third.shape[1])
    near = pack_call(
        "pack_near", core_at, wide, [(up_own, up_came)], [down_weight, out_weight]
    )
    far = pack_call(
        "pack_far",
        core_at,
        narrow,
        [(first_own, first_came)],
        [tap_third, later(tap_second, qkv_have[1])],
        chips,
    )
    near_have = {0: later(near, modulation)}
    pull(near_have, 1, 0)
    near_own = [near_have[1 << b] for b in range(bits)]

    tile = 256 if rows % 512 == 0 else rows // 2
    heads = HEADS // 2
    tokens = jnp.concatenate([tokens_own, flip_core(tokens_own)])
    head_shape = (heads, rows, HEAD_DIM)
    inner = heads * HEAD_DIM
    hidden_ff = up_weight.shape[1] // 2
    tap_width = tap_first.shape[1] // 2
    tap_out = tap_third.shape[1]

    def flat(columns, dtype):
        return ((rows, columns), dtype, 0)

    def turned(columns):
        return ((columns, rows), HALF, 1)

    call = functools.partial(token_call, rows=rows, tile=tile)
    hidden_one_t, query, key, value = call(
        "qkv",
        qkv_body,
        me,
        [(tokens, False)],
        [shift_one, scale_one, qkv_bias_own],
        [qkv_weights],
        [turned(width)] + [(head_shape, HALF, 1)] * 3,
        [],
    )
    context, lse = attention_call(query, key, value)
    for r in [r for r in near_have if r]:
        near_have[r] = later(near_have[r], "attention")
    far_have = {0: far}
    height, high = 2 * up_own.shape[0], tap_second.shape[0]
    columns, tap_columns = up_own.shape[1], first_own.shape[1]
    cut = height * columns // wide
    (up_places, mixed_places), (up_last, _) = pull_parts(near_have, cut)
    up_weights = stacked_weight(up_places, 0, wide, columns, height)
    down_weights = stacked_weight(mixed_places, 0, wide, wide, down_weight.shape[0])
    out_weights = stacked_weight(
        mixed_places, down_weight.shape[0], wide, wide, out_weight.shape[0]
    )
    for bit in range(bits):
        far_have[1 << bit] = flip_chip(later(far, *near_own), bit)
    cut = height * tap_columns // narrow + high * tap_third.shape[1] // narrow
    (first_places, second_places), _ = pull_parts(far_have, cut)
    first_weights = stacked_weight(first_places, 0, narrow, tap_columns, height)
    third_weights = stacked_weight(
        first_places, height * tap_columns // narrow, narrow, tap_third.shape[1], high
    )
    second_weights = stacked_weight(second_places, 0, narrow, tap_second.shape[1], high)

    beside_pieces = to_chip(
        later(jnp.concatenate([cotangent, targets], axis=2), "qkv"), 1
    )
    beside = jnp.concatenate(beside_pieces)
    out_part, out_low, context_t = call(
        "out",
        out_body,
        me,
        [(context, False)],
        [],
        [out_weights],
        [flat(width, WIDE), flat(width, HALF), turned(inner)],
        [],
        after=[*up_last, far, beside_pieces[1]],
    )
    out_came = flip_core(out_low)
    mixed, hidden_two_t, upper, act_t, feed_part, feed_low = call(
        "feed",
        feed_body,
        me,
        [(tokens, False), (out_part, False), (out_came, True)],
        [gate_one, shift_two, scale_two, out_bias_full, up_bias_own],
        [up_weights, down_weights],
        [
            flat(width, WIDE),
            turned(width),
            flat(hidden_ff, WIDE),
            turned(hidden_ff),
            flat(width, WIDE),
            flat(width, HALF),
        ],
        [],
        after=[beside, *[far_have[1 << b] for b in range(bits)]],
    )
    feed_came = flip_core(feed_low)
    beside_all = jnp.concatenate([beside, flip_core(beside)])
    cotangent_all, targets_all = beside_all[:, :width], beside_all[:, width:]
    block_out, block_t, first_pre, first_t, second_part, second_low = call(
        "tap",
        tap_body,
        me,
        [(mixed, False), (feed_part, False), (feed_came, True)],
        [gate_two, down_bias_full, first_bias_own],
        [first_weights, second_weights],
        [
            flat(width, HALF),
            turned(width),
            flat(tap_width, WIDE),
            turned(tap_width),
            flat(tap_width, WIDE),
            flat(tap_width, HALF),
        ],
        [],
    )
    second_came = flip_core(second_low)
    second_pre, second_t, latent_part, latent_low = call(
        "latent",
        latent_body,
        me,
        [(second_part, False), (second_came, True)],
        [second_bias_own],
        [third_weights],
        [flat(tap_width, WIDE), turned(tap_width), flat(tap_out, WIDE), flat(tap_out, HALF)],
        [],
    )
    latent_came = flip_core(latent_low)

    dlatent, dsecond, cos_sum, third_bg, second_bg = call(
        "cosine",
        cosine_body,
        me,
        [(latent_part, False), (latent_came, True), (targets_all, False), (second_pre, False)],
        [third_bias_full],
        [third_weights],
        [flat(tap_out, HALF), flat(tap_width, HALF)],
        [(1, 128), (1, tap_out), (1, tap_width)],
    )
    dsecond_came = flip_core(dsecond)
    third_plan = [(ranks(1 % bits), 0, tap_third.shape[0])]
    third_wg = weight_grad_call("third_grad", me, second_t, [dlatent], third_plan, 384)
    second_plan = [(ranks(0), 0, tap_second.shape[0])]
    second_wg = weight_grad_call(
        "second_grad", me, first_t, [dsecond, dsecond_came], second_plan, 512, after=third_wg[:1]
    )
    dfirst, tap_part, tap_low, first_bg = call(
        "tap_back",
        tap_back_body,
        me,
        [(dsecond, False), (dsecond_came, True), (first_pre, False)],
        [],
        [second_weights, first_weights],
        [flat(tap_width, HALF), flat(width, WIDE), flat(width, HALF)],
        [(1, tap_width)],
        after=[second_wg[0]],
    )
    tap_came = flip_core(tap_low)
    block_output, block_pieces = from_chip(
        block_out[: rows // 2], 2, (("cosine",), ("cosine",), ("tap_back",), ("tap_back",))
    )
    third_sent, third_far = scatter_begin(third_wg, third_plan, "tap_back")
    first_plan = [(ranks(1 % bits), 0, height)]
    first_wg = weight_grad_call(
        "first_grad", me, block_t, [dfirst], first_plan, 512, after=third_far + block_pieces[:2]
    )
    doutput, dfeed, dupper, hidden_part, hidden_low, gate_two_grad, down_bg, up_bg = call(
        "feed_back",
        feed_back_body,
        me,
        [
            (cotangent_all, False),
            (tap_part, False),
            (tap_came, True),
            (feed_part, False),
            (feed_came, True),
            (upper, False),
        ],
        [gate_two, down_bias_full],
        [down_weights, up_weights],
        [
            flat(width, WIDE),
            flat(width, HALF),
            flat(hidden_ff, HALF),
            flat(width, WIDE),
            flat(width, HALF),
        ],
        [(1, width), (1, width), (1, hidden_ff)],
        after=[first_wg[0], *block_pieces],
    )

    second_sent, second_far = scatter_begin(second_wg, second_plan, "feed_back")
    first_sent, first_far = scatter_begin(first_wg, first_plan, "feed_back")
    third_part = scatter_end(third_sent, "feed_back")
    hidden_came = flip_core(hidden_low)
    down_plan = halves(down_weight.shape[0])
    down_wg = weight_grad_call(
        "down_grad", me, act_t, [dfeed], down_plan, 384, after=first_far
    )
    up_plan = halves(height)
    up_wg = weight_grad_call(
        "up_grad", me, hidden_two_t, [dupper], up_plan, 384, after=[down_wg[0], *second_far]
    )
    first_sum = scatter_end(first_sent, "up_grad")
    second_sum = scatter_end(second_sent, "up_grad")
    third_part = lax.psum(third_part, "seq")
    first_sum = lax.psum(later(first_sum, third_part), "seq")
    (
        dmixed,
        dattended,
        dcontext,
        shift_two_grad,
        scale_two_grad,
        gate_one_grad,
        out_bg,
    ) = call(
        "mix_back",
        mix_back_body,
        me,
        [
            (mixed, False),
            (doutput, False),
            (hidden_part, False),
            (hidden_came, True),
            (out_part, False),
            (out_came, True),
        ],
        [scale_two, gate_one, out_bias_full],
        [out_weights],
        [flat(width, WIDE), flat(width, HALF), (head_shape, HALF, 1)],
        [(1, width)] * 4,
        after=[up_wg[0], third_part],
    )
    down_sent, down_far = scatter_begin(down_wg, down_plan, "mix_back")
    out_plan = [(ranks(0), 0, out_weight.shape[0])]
    out_wg = weight_grad_call(
        "out_grad", me, context_t, [dattended], out_plan, 384
    )
    dquery, dkey, dvalue = attention_back_call(
        query, key, value, dcontext, lse, after=[out_wg[0], *[parts[-1] for parts in down_sent]]
    )
    second_sum = lax.psum(later(second_sum, first_sum, "out_grad"), "seq")
    up_sent, up_far = scatter_begin(up_wg, up_plan, "attention_back")
    dqkv, one_part, one_low, qkv_bg = call(
        "qkv_back",
        qkv_back_body,
        me,
        [(dquery, False), (dkey, False), (dvalue, False)],
        [],
        [qkv_weights],
        [flat(3 * inner, HALF), flat(width, WIDE), flat(width, HALF)],
        [(1, 3 * inner)],
        after=[first_sum, *up_far],
    )
    one_came = flip_core(one_low[rows // 2 :])
    qkv_plan = halves(qkv_have[0].shape[0])
    out_sent, out_far = scatter_begin(out_wg, out_plan, "qkv_back")
    qkv_wg = weight_grad_call(
        "qkv_grad", me, hidden_one_t, [dqkv], qkv_plan, 384
    )
    up_part = scatter_end(up_sent, "qkv_grad")
    out_part = scatter_end(out_sent, "qkv_grad")
    down_part = scatter_end(down_sent, "attention_back")
    down_part = lax.psum(later(down_part, second_sum), "seq")
    up_part, out_part = lax.psum((later(up_part, down_part), out_part), "seq")
    input_low, shift_one_grad, scale_one_grad = token_call(
        "input_grad",
        input_body,
        me,
        [(tokens, False), (dmixed, False), (one_part, False), (one_came, False)],
        [scale_one],
        [],
        [((rows // 2, width), HALF, 0)],
        [(1, width)] * 2,
        rows=rows // 2,
        tile=tile,
        after=[qkv_wg[0], second_sum, *out_far],
    )
    input_grad = from_chip(input_low, 2)[0].astype(WIDE)

    qkv_sent, qkv_far = scatter_begin(qkv_wg, qkv_plan, "input_grad")
    qkv_scattered = scatter_end(qkv_sent)
    qkv_hops = []
    qkv_part = sum_planes(qkv_scattered, qkv_hops)
    one_grads = jnp.concatenate([shift_one_grad, scale_one_grad], axis=1)
    one_grads = later(one_grads + flip_core(one_grads), *qkv_far)
    modulation_grad = jnp.concatenate(
        [one_grads, gate_one_grad, shift_two_grad, scale_two_grad, gate_two_grad], axis=1
    )
    for bit in range(bits):
        modulation_grad = jnp.concatenate([modulation_grad, flip_chip(modulation_grad, bit)])
    for bit in range(n_seq.bit_length() - 1):
        modulation_grad = jnp.concatenate([modulation_grad, flip_plane(modulation_grad, bit)])
    nth = jnp.arange(chips * n_seq)
    picked = ((nth % chips) ^ chip) * n_seq + ((nth // chips) ^ plane)
    pick = (picked[:, None] == jnp.arange(chips * n_seq)[None, :]).astype(WIDE)
    modulation_all = later(jnp.dot(pick.T, modulation_grad, precision=HIGH), qkv_hops[-1])
    ada_wg = jnp.einsum(
        "bi,bj->ij", cond_low.astype(WIDE), modulation_all, precision=HIGH
    )
    ada_size = ada_bias.shape[0]
    ada_bg = lax.dynamic_slice(jnp.sum(modulation_all, axis=0), (place * ada_size,), (ada_size,))
    cond_grad = cond_back(
        jnp.einsum("bj,ij->bi", modulation_all, ada_low.astype(WIDE), precision=HIGH)
    )[0]
    cond_grad = lax.all_gather(cond_grad, "dp", axis=1, tiled=True)
    time_hot = (
        bucket_all[:, None] == jnp.arange(time_table.shape[0], dtype=jnp.int32)[None, :]
    ).astype(WIDE)
    class_hot = (
        labels_all[:, None] == jnp.arange(class_table.shape[0], dtype=jnp.int32)[None, :]
    ).astype(WIDE)
    time_grad = jnp.einsum("bt,bd->td", time_hot, cond_grad, precision=HIGH)
    class_grad = jnp.einsum("bt,bd->td", class_hot, cond_grad, precision=HIGH)

    sums = [qkv_bg, up_bg, first_bg, second_bg, out_bg, down_bg, third_bg, cos_sum]
    line = later(jnp.concatenate(sums, axis=1), *qkv_far)
    for bit in range(bits):
        line = line + flip_chip(line, bit)
    for bit in range(n_seq.bit_length() - 1):
        line = line + flip_plane(line, bit)
    split_at = sum(s.shape[1] for s in sums[:4])
    came = flip_core(line[:, :split_at])
    bias_grads, at = [], 0
    for k, (item, groups) in enumerate(zip(sums[:4], (3, 1, 1, 1))):
        size = item.shape[1]
        bias_grads.append(
            from_cores(line[:, at : at + size], came[:, at : at + size], groups)
        )
        at += size
    for item in sums[4:7]:
        bias_grads.append(line[:, at : at + item.shape[1]])
        at += item.shape[1]
    align_loss = -0.5 * line[:, at : at + 1] / (rows * chips * n_seq)

    def own_part(grad):
        size = grad.shape[1] // n_dp
        return lax.dynamic_slice(grad, (0, place * size), (1, size))[0]

    qkv_bo, up_bo, first_bo, second_bo, out_bo, down_bo, third_bo = map(own_part, bias_grads)

    def whole_columns(grad, groups):
        size = grad.shape[0] // 2
        own = lax.dynamic_slice(grad, (core * size, 0), (size, grad.shape[1]))
        other = lax.dynamic_slice(grad, ((1 - core) * size, 0), (size, grad.shape[1]))
        return join_call("join", core_at, own, flip_core(other), groups, chips)

    block_output = later(block_output, "input_grad")
    third_part, second_sum, first_sum, down_part, up_part, out_part = (
        later(a, "input_grad", qkv_scattered)
        for a in (third_part, second_sum, first_sum, down_part, up_part, out_part)
    )
    third_own = third_part.astype(WIDE)
    second_own = join_call(
        "join", core_at, second_sum[:, :tap_width], second_sum[:, tap_width:], 1, chips
    )
    first_own = whole_columns(first_sum, 1)
    down_own = down_part.astype(WIDE)
    up_own = whole_columns(up_part, 1)
    out_own = out_part.astype(WIDE)
    qkv_own = whole_columns(qkv_part, 3)
    align_loss = last_call(align_loss, spent)[0, 0]
    return (
        block_output,
        input_grad,
        align_loss,
        time_grad,
        class_grad,
        ada_wg,
        ada_bg,
        qkv_own,
        qkv_bo,
        out_own,
        out_bo,
        up_own,
        up_bo,
        down_own,
        down_bo,
        first_own,
        first_bo,
        second_own,
        second_bo,
        third_own,
        third_bo,
    )


def solution(mesh):
    tokens, rows, line = P("dp", "seq", None), P("dp", None), P("dp")
    return jax.shard_map(
        functools.partial(shards, mesh.shape["dp"], mesh.shape["seq"]),
        mesh=mesh,
        in_specs=(tokens, tokens, tokens, line, line, P(), P()) + (rows, line) * 8,
        out_specs=(tokens, tokens, P(), P(), P()) + (rows, line) * 8,
        check_vma=False,
    )
```

```python
import functools
import math

import jax
import jax.numpy as jnp
from jax import lax
from jax.experimental import pallas as pl
from jax.experimental.pallas import tpu as pltpu
from jax.sharding import PartitionSpec as P

HEADS = 16
HEAD_DIM = 72
EPS_NORM = 1e-06
HIGH = lax.Precision.HIGHEST
HALF = jnp.bfloat16
WIDE = jnp.float32
VMEM_BYTES = 56 * 1024 * 1024
GELU_A = math.sqrt(2.0 / math.pi)
GELU_B = 0.044715
SCALE = 1
MARK = (8, 128)
DONE = {}
TAKES = {
    "qkv": 13,
    "attention": 30,
    "out": 8,
    "feed": 27,
    "tap": 16,
    "latent": 9,
    "cosine": 9,
    "tap_back": 16,
    "third_grad": 5,
    "second_grad": 8,
    "first_grad": 6,
    "feed_back": 28,
    "down_grad": 12,
    "up_grad": 12,
    "mix_back": 14,
    "out_grad": 5,
    "attention_back": 31,
    "qkv_back": 12,
    "qkv_grad": 10,
    "input_grad": 5,
    "split_qkv": 3,
    "split_rest": 3,
    "pack_near": 4,
    "pack_far": 4,
    "condition": 2,
}


def cost(microseconds):
    return pl.CostEstimate(
        flops=int(microseconds * SCALE * 1.15e9),
        bytes_accessed=int(microseconds * SCALE * 3.6e6),
        transcendentals=0,
    )


def dot(left, right):
    return jnp.dot(left, right, preferred_element_type=WIDE)


def dot_nt(left, right):
    return lax.dot_general(left, right, (((1,), (1,)), ((), ())), preferred_element_type=WIDE)


def normed(values):
    centre = values - jnp.mean(values, axis=-1, keepdims=True)
    spread = jnp.mean(centre * centre, axis=-1, keepdims=True)
    inverse = lax.rsqrt(spread + EPS_NORM)
    return centre * inverse, inverse


def normed_back(norm, inverse, grad):
    return (
        grad
        - jnp.mean(grad, axis=-1, keepdims=True)
        - norm * jnp.mean(grad * norm, axis=-1, keepdims=True)
    ) * inverse


def sigmoid(values):
    return 1.0 / (1.0 + jnp.exp(-values))


def silu_back(pre, grad):
    gate = sigmoid(pre)
    return grad * (gate * (1.0 + pre * (1.0 - gate)))


def gelu(values):
    inner = jnp.tanh(GELU_A * (values + GELU_B * (values * values * values)))
    return 0.5 * values * (1.0 + inner)


def gelu_back(values, grad):
    square = values * values
    inner = jnp.tanh(GELU_A * (values + GELU_B * (square * values)))
    slope = 0.5 * (1.0 + inner) + 0.5 * values * (1.0 - inner * inner) * (
        GELU_A * (1.0 + 3.0 * GELU_B * square)
    )
    return grad * slope


def total(values):
    return jnp.sum(values, axis=0, keepdims=True)


def spans(size, most):
    count = -(-size // most)
    while size % count or (size // count) % 128:
        count += 1
        if count > size // 128:
            return [(0, size)]
    return [(k * (size // count), size // count) for k in range(count)]


def joined(ref, index=slice(None)):
    return jnp.concatenate([ref[h] for h in range(ref.shape[0])], axis=-1)


class Weight:
    def __init__(self, me, step, arrays, how, store, sems):
        self.me, self.step, self.arrays, self.how = me, step, arrays, how
        self.store, self.sems = store, sems

    def copies(self):
        groups, by_me, height, _ = self.how
        count = 0
        for places, pieces in groups:
            for r, (number, base) in enumerate(places):
                start = pl.multiple_of((self.me ^ r) * height, height) if by_me else r * height
                for row, rows, column, columns, to_row, to_column in pieces:
                    yield pltpu.make_async_copy(
                        self.arrays[number].at[pl.ds(base + row, rows), pl.ds(column, columns)],
                        self.store.at[pl.ds(start + to_row, rows), pl.ds(to_column, columns)],
                        self.sems.at[count],
                    )
                    count += 1

    def start(self):
        @pl.when(self.step == 0)
        def _():
            for copy in self.copies():
                copy.start()

    def ready(self):
        @pl.when(self.step == 0)
        def _():
            for copy in self.copies():
                copy.wait()

        return self.store


def token_kernel(body, counts, hows, me_ref, *refs):
    n_tok, n_const, n_blocks, n_after, n_out, n_sum = counts
    refs = list(refs)
    take = lambda n: [refs.pop(0) for _ in range(n)]
    toks, consts = take(n_tok), take(n_const)
    blocks = [take(n) for n in n_blocks]
    take(n_after)
    outs, sums, (mark,) = take(n_out), take(n_sum), take(1)
    step = pl.program_id(0)

    @pl.when(step == 0)
    def _():
        mark[...] = jnp.zeros_like(mark)

    weights = [
        Weight(me_ref[0], step, group, hows[k], refs[2 * k], refs[2 * k + 1])
        for k, group in enumerate(blocks)
    ]
    for weight in weights:
        weight.start()
    if sums:

        @pl.when(step == 0)
        def _():
            for ref in sums:
                ref[...] = jnp.zeros_like(ref)

    body(toks, consts, weights, outs, sums)


def token_call(name, body, me, toks, consts, weights, outs, sums, rows, tile, after=()):
    steps = rows // tile

    def spec(shape, dim, swapped=False):
        block = tuple(tile if k == dim else s for k, s in enumerate(shape))

        def place(i, me_ref):
            at = lax.rem(i + steps // 2, steps) if swapped else i
            return tuple(at if k == dim else 0 for k in range(len(shape)))

        return pl.BlockSpec(block, place)

    def whole(shape):
        return pl.BlockSpec(shape, lambda i, me_ref: (0,) * len(shape))

    in_specs = [spec(a.shape, a.ndim - 2, swapped) for a, swapped in toks]
    in_specs += [whole(c.shape) for c in consts]
    blocks = [array for group, _ in weights for array in group]
    in_specs += [pl.BlockSpec(memory_space=pl.ANY)] * (len(blocks) + len(after))
    out_specs = [spec(shape, dim) for shape, _, dim in outs] + [whole(shape) for shape in sums]
    out_shape = [jax.ShapeDtypeStruct(shape, dtype) for shape, dtype, _ in outs]
    out_shape += [jax.ShapeDtypeStruct(shape, WIDE) for shape in sums]
    out_specs.append(whole(MARK))
    out_shape.append(jax.ShapeDtypeStruct(MARK, WIDE))
    scratch = []
    for _, (groups, _, height, columns) in weights:
        scratch += [
            pltpu.VMEM((height * len(groups[0][0]), columns), HALF),
            pltpu.SemaphoreType.DMA((sum(len(a) * len(b) for a, b in groups),)),
        ]
    counts = (len(toks), len(consts), [len(g) for g, _ in weights], len(after), len(outs), len(sums))
    *found, DONE[name] = pl.pallas_call(
        functools.partial(token_kernel, body, counts, [how for _, how in weights]),
        grid_spec=pltpu.PrefetchScalarGridSpec(
            num_scalar_prefetch=1,
            grid=(steps,),
            in_specs=in_specs,
            out_specs=out_specs,
            scratch_shapes=scratch,
        ),
        out_shape=out_shape,
        compiler_params=pltpu.CompilerParams(
            dimension_semantics=("arbitrary",), vmem_limit_bytes=VMEM_BYTES
        ),
        cost_estimate=cost(TAKES[name]),
        name=name,
    )(me, *[a for a, _ in toks], *consts, *blocks, *after)
    return found


def qkv_body(toks, consts, weights, outs, sums):
    (x,), (shift, scale, bias), (weight,) = toks, consts, weights
    hidden_t, query, key, value = outs
    norm, _ = normed(x[...].astype(WIDE))
    hidden = norm * (1.0 + scale[...]) + shift[...]
    low = hidden.astype(HALF)
    hidden_t[...] = hidden.T.astype(HALF)
    store = weight.ready()
    width = store.shape[1] // 3
    for k, out in enumerate((query, key, value)):
        part = dot(low, store[:, k * width : (k + 1) * width])
        part = (part + bias[:, k * width : (k + 1) * width]).astype(HALF)
        for h in range(out.shape[0]):
            out[h] = part[:, h * HEAD_DIM : (h + 1) * HEAD_DIM]


def attention_kernel(query, key, value, *refs):
    context, lse, mark = refs[-3:]
    mark[...] = jnp.zeros_like(mark)
    factor = 1.0 / math.sqrt(HEAD_DIM)
    keys, values = key[0], value[0]
    rows = query.shape[1]
    tile = min(rows, 256)
    for start in range(0, rows, tile):
        at = slice(start, start + tile)
        scores = dot_nt(keys, query[0, at, :]) * factor
        highest = jnp.max(scores, axis=0, keepdims=True)
        expo = jnp.exp(scores - highest)
        summed = jnp.sum(expo, axis=0, keepdims=True)
        probs = (expo / summed).astype(HALF)
        lse[0, :, at] = highest + jnp.log(summed)
        found = lax.dot_general(
            values, probs, (((0,), (0,)), ((), ())), preferred_element_type=WIDE
        )
        context[0, at, :] = found.T.astype(HALF)


def attention_call(query, key, value, after=()):
    heads, rows, _ = query.shape
    block = pl.BlockSpec((1, rows, HEAD_DIM), lambda h: (h, 0, 0))
    line = pl.BlockSpec((1, 1, rows), lambda h: (h, 0, 0))
    *found, DONE["attention"] = pl.pallas_call(
        attention_kernel,
        grid=(heads,),
        in_specs=[block] * 3 + [pl.BlockSpec(memory_space=pl.ANY)] * len(after),
        out_specs=[block, line, pl.BlockSpec(MARK, lambda h: (0, 0))],
        out_shape=[
            jax.ShapeDtypeStruct(query.shape, HALF),
            jax.ShapeDtypeStruct((heads, 1, rows), WIDE),
            jax.ShapeDtypeStruct(MARK, WIDE),
        ],
        compiler_params=pltpu.CompilerParams(
            dimension_semantics=("arbitrary",), vmem_limit_bytes=VMEM_BYTES
        ),
        cost_estimate=cost(TAKES["attention"]),
        name="attention",
    )(query, key, value, *after)
    return found


def attention_back_kernel(query, key, value, grad, lse, *refs):
    dquery, dkey, dvalue, mark, sum_key, sum_value = refs[-6:]
    mark[...] = jnp.zeros_like(mark)
    factor = 1.0 / math.sqrt(HEAD_DIM)
    keys, values = key[0], value[0]
    rows = query.shape[1]
    tile = min(rows, 256)
    for start in range(0, rows, tile):
        at = slice(start, start + tile)
        queries, grads = query[0, at, :], grad[0, at, :]
        probs = jnp.exp(dot_nt(keys, queries) * factor - lse[0, :, at])
        dprobs = dot_nt(values, grads)
        held = jnp.sum(probs * dprobs, axis=0, keepdims=True)
        dscores = (probs * (dprobs - held)).astype(HALF)
        value_part = dot(probs.astype(HALF), grads)
        key_part = dot(dscores, queries)
        if start == 0:
            sum_value[...] = value_part
            sum_key[...] = key_part
        else:
            sum_value[...] += value_part
            sum_key[...] += key_part
        found = lax.dot_general(
            keys, dscores, (((0,), (0,)), ((), ())), preferred_element_type=WIDE
        )
        dquery[0, at, :] = (found * factor).T.astype(HALF)
    dkey[0] = (sum_key[...] * factor).astype(HALF)
    dvalue[0] = sum_value[...].astype(HALF)


def attention_back_call(query, key, value, grad, lse, after=()):
    heads, rows, _ = query.shape
    block = pl.BlockSpec((1, rows, HEAD_DIM), lambda h: (h, 0, 0))
    line = pl.BlockSpec((1, 1, rows), lambda h: (h, 0, 0))
    *found, DONE["attention_back"] = pl.pallas_call(
        attention_back_kernel,
        grid=(heads,),
        in_specs=[block] * 4 + [line] + [pl.BlockSpec(memory_space=pl.ANY)] * len(after),
        out_specs=[block] * 3 + [pl.BlockSpec(MARK, lambda h: (0, 0))],
        out_shape=[jax.ShapeDtypeStruct(query.shape, HALF)] * 3
        + [jax.ShapeDtypeStruct(MARK, WIDE)],
        scratch_shapes=[pltpu.VMEM((rows, HEAD_DIM), WIDE)] * 2,
        compiler_params=pltpu.CompilerParams(
            dimension_semantics=("arbitrary",), vmem_limit_bytes=VMEM_BYTES
        ),
        cost_estimate=cost(TAKES["attention_back"]),
        name="attention_back",
    )(query, key, value, grad, lse, *after)
    return found


def out_body(toks, consts, weights, outs, sums):
    (context,), (weight,) = toks, weights
    part, low, context_t = outs
    heads = joined(context)
    context_t[...] = heads.astype(WIDE).T.astype(HALF)
    found = dot(heads, weight.ready()[...])
    part[...] = found
    low[...] = found.astype(HALF)


def feed_body(toks, consts, weights, outs, sums):
    x, part, other = toks
    gate_one, shift, scale, out_bias, up_bias = consts
    up, down = weights
    mixed, hidden_t, upper, act_t, feed, feed_low = outs
    attended = part[...] + other[...].astype(WIDE) + out_bias[...]
    mix = x[...].astype(WIDE) + gate_one[...] * attended
    mixed[...] = mix
    norm, _ = normed(mix)
    hidden = norm * (1.0 + scale[...]) + shift[...]
    low = hidden.astype(HALF)
    hidden_t[...] = hidden.T.astype(HALF)
    up_store = up.ready()
    acc = None
    for k, (start, size) in enumerate(spans(up_store.shape[1], 768)):
        at = slice(start, start + size)
        pre = dot(low, up_store[:, at]) + up_bias[:, at]
        upper[:, at] = pre
        act = gelu(pre)
        act_t[at, :] = act.T.astype(HALF)
        if k == 0:
            down_store = down.ready()
        term = dot(act.astype(HALF), down_store[at, :])
        acc = term if acc is None else acc + term
    feed[...] = acc
    feed_low[...] = acc.astype(HALF)


def tap_body(toks, consts, weights, outs, sums):
    mixed, part, other = toks
    gate_two, down_bias, first_bias = consts
    first, second = weights
    block_out, block_t, first_pre, first_t, own, sent = outs
    feed = part[...] + other[...].astype(WIDE) + down_bias[...]
    output = mixed[...] + gate_two[...] * feed
    low = output.astype(HALF)
    block_out[...] = low
    block_t[...] = output.T.astype(HALF)
    pre = dot(low, first.ready()[...]) + first_bias[...]
    first_pre[...] = pre
    act = pre * sigmoid(pre)
    first_t[...] = act.T.astype(HALF)
    act_low = act.astype(HALF)
    store = second.ready()
    half = store.shape[1] // 2
    own[...] = dot(act_low, store[:, :half])
    sent[...] = dot(act_low, store[:, half:]).astype(HALF)


def latent_body(toks, consts, weights, outs, sums):
    (part, other), (bias,), (third,) = toks, consts, weights
    second_pre, second_t, own, low = outs
    pre = part[...] + other[...].astype(WIDE) + bias[...]
    second_pre[...] = pre
    act = pre * sigmoid(pre)
    second_t[...] = act.T.astype(HALF)
    found = dot(act.astype(HALF), third.ready()[...])
    own[...] = found
    low[...] = found.astype(HALF)


def cosine_body(toks, consts, weights, outs, sums):
    part, other, targets, second_pre = toks
    (bias,), (third,) = consts, weights
    dlatent, dsecond = outs
    cos_sum, third_bias_sum, second_bias_sum = sums
    latent = part[...] + other[...].astype(WIDE) + bias[...]
    target = targets[...].astype(WIDE)
    inner = jnp.sum(latent * target, axis=-1, keepdims=True)
    length = jnp.sum(latent * latent, axis=-1, keepdims=True) + EPS_NORM
    inverse = lax.rsqrt(length)
    inverse_target = lax.rsqrt(jnp.sum(target * target, axis=-1, keepdims=True) + EPS_NORM)
    cos = inner * inverse * inverse_target
    cos_sum[...] += jnp.broadcast_to(total(cos), cos_sum.shape)
    low = (-0.5 * (target * (inverse * inverse_target) - latent * (cos / length))).astype(HALF)
    dlatent[...] = low
    third_bias_sum[...] += total(low.astype(WIDE))
    pre_grad = silu_back(second_pre[...], dot_nt(low, third.ready()[...])).astype(HALF)
    dsecond[...] = pre_grad
    second_bias_sum[...] += total(pre_grad.astype(WIDE))


def tap_back_body(toks, consts, weights, outs, sums):
    own, other, first_pre = toks
    second, first = weights
    dfirst, part, low = outs
    (bias_sum,) = sums
    grads = jnp.concatenate([own[...], other[...]], axis=-1)
    pre_grad = silu_back(first_pre[...], dot_nt(grads, second.ready()[...])).astype(HALF)
    dfirst[...] = pre_grad
    bias_sum[...] += total(pre_grad.astype(WIDE))
    found = dot_nt(pre_grad, first.ready()[...])
    part[...] = found
    low[...] = found.astype(HALF)


def feed_back_body(toks, consts, weights, outs, sums):
    cotangent, part, other, feed_part, feed_other, upper = toks
    gate_two, down_bias = consts
    down, up = weights
    doutput, dfeed, dupper, hidden, hidden_low = outs
    gate_sum, down_bias_sum, up_bias_sum = sums
    grad = cotangent[...].astype(WIDE) + part[...] + other[...].astype(WIDE)
    doutput[...] = grad
    feed = feed_part[...] + feed_other[...].astype(WIDE) + down_bias[...]
    gate_sum[...] += total(grad * feed)
    low = (grad * gate_two[...]).astype(HALF)
    dfeed[...] = low
    down_bias_sum[...] += total(low.astype(WIDE))
    down_store = down.ready()
    acc = None
    for k, (start, size) in enumerate(spans(down_store.shape[0], 768)):
        at = slice(start, start + size)
        pre_grad = gelu_back(upper[:, at], dot_nt(low, down_store[at, :])).astype(HALF)
        dupper[:, at] = pre_grad
        up_bias_sum[:, at] += total(pre_grad.astype(WIDE))
        if k == 0:
            up_store = up.ready()
        term = dot_nt(pre_grad, up_store[:, at])
        acc = term if acc is None else acc + term
    hidden[...] = acc
    hidden_low[...] = acc.astype(HALF)


def mix_back_body(toks, consts, weights, outs, sums):
    mixed, doutput, part, other, out_part, out_other = toks
    scale, gate_one, out_bias = consts
    (weight,) = weights
    dmixed, dattended, dcontext = outs
    shift_sum, scale_sum, gate_sum, bias_sum = sums
    grad = part[...] + other[...].astype(WIDE)
    norm, inverse = normed(mixed[...])
    shift_sum[...] += total(grad)
    scale_sum[...] += total(grad * norm)
    mix_grad = doutput[...] + normed_back(norm, inverse, grad * (1.0 + scale[...]))
    dmixed[...] = mix_grad
    attended = out_part[...] + out_other[...].astype(WIDE) + out_bias[...]
    gate_sum[...] += total(mix_grad * attended)
    low = (mix_grad * gate_one[...]).astype(HALF)
    dattended[...] = low
    bias_sum[...] += total(low.astype(WIDE))
    found = dot_nt(low, weight.ready()[...]).astype(HALF)
    for h in range(dcontext.shape[0]):
        dcontext[h] = found[:, h * HEAD_DIM : (h + 1) * HEAD_DIM]


def qkv_back_body(toks, consts, weights, outs, sums):
    (weight,) = weights
    grads, part, low = outs
    (bias_sum,) = sums
    row = jnp.concatenate([joined(ref) for ref in toks], axis=-1)
    grads[...] = row
    bias_sum[...] += total(row.astype(WIDE))
    found = dot_nt(row, weight.ready()[...])
    part[...] = found
    low[...] = found.astype(HALF)


def input_body(toks, consts, weights, outs, sums):
    x, dmixed, part, other = toks
    (scale,) = consts
    (found,) = outs
    shift_sum, scale_sum = sums
    grad = part[...] + other[...].astype(WIDE)
    norm, inverse = normed(x[...].astype(WIDE))
    shift_sum[...] += total(grad)
    scale_sum[...] += total(grad * norm)
    result = dmixed[...] + normed_back(norm, inverse, grad * (1.0 + scale[...]))
    found[...] = result.astype(HALF)


def weight_grad_kernel(plan, size, sides, me_ref, left, *refs):
    count = 2 * len(plan)
    rights, (*outs, mark, hold) = refs[:sides], refs[-2 - count :]
    mark[...] = jnp.zeros_like(mark)

    def emit(found):
        hold[...] = found.astype(hold.dtype)
        for (ranks, row, rows), near, far in zip(plan, outs[::2], outs[1::2]):
            for k, r in enumerate(ranks):
                start = pl.multiple_of((me_ref[0] ^ r) * size + row, math.gcd(size, row or size))
                out = near if k < len(ranks) // 2 else far
                at = k % (len(ranks) // 2) * rows
                out[at : at + rows, :] = hold[pl.ds(start, rows), :].astype(HALF)

    if sides == 1:
        emit(dot(left[...], rights[0][...]))
        return
    is_own = pl.program_id(0) < pl.num_programs(0) // 2

    @pl.when(is_own)
    def _():
        emit(dot(left[...], rights[0][...]))

    @pl.when(jnp.logical_not(is_own))
    def _():
        half = left.shape[1] // 2
        emit(
            dot(left[:, :half], rights[1][half:, :]) + dot(left[:, half:], rights[1][:half, :])
        )


def weight_grad_call(name, me, left, rights, plan, tile, after=()):
    features, rows = left.shape
    columns = rights[0].shape[1]
    sides = len(rights)
    size = features // len(plan[0][0])
    tile = min(tile, columns)
    steps = pl.cdiv(columns, tile)
    hold = HALF if all(row % 16 == 0 and part % 16 == 0 for _, row, part in plan) else WIDE
    assert sides == 1 or columns % tile == 0
    outs = [(part * len(ranks) // 2, sides * columns) for ranks, _, part in plan for _ in range(2)]
    *found, DONE[name] = pl.pallas_call(
        functools.partial(weight_grad_kernel, plan, size, sides),
        grid_spec=pltpu.PrefetchScalarGridSpec(
            num_scalar_prefetch=1,
            grid=(sides * steps,),
            in_specs=[
                pl.BlockSpec((features, rows), lambda n, me_ref: (0, 0)),
                pl.BlockSpec((rows, tile), lambda n, me_ref: (0, jnp.minimum(n, steps - 1))),
                pl.BlockSpec((rows, tile), lambda n, me_ref: (0, jnp.maximum(n - steps, 0))),
            ][: 1 + sides]
            + [pl.BlockSpec(memory_space=pl.ANY)] * len(after),
            out_specs=[pl.BlockSpec((o[0], tile), lambda n, me_ref: (0, n)) for o in outs]
            + [pl.BlockSpec(MARK, lambda n, me_ref: (0, 0))],
            scratch_shapes=[pltpu.VMEM((features, tile), hold)],
        ),
        out_shape=[jax.ShapeDtypeStruct(o, HALF) for o in outs]
        + [jax.ShapeDtypeStruct(MARK, WIDE)],
        compiler_params=pltpu.CompilerParams(
            dimension_semantics=("arbitrary",), vmem_limit_bytes=VMEM_BYTES
        ),
        cost_estimate=cost(TAKES[name]),
        name=name,
    )(me, left, *rights, *after)
    return found


def split_kernel(plan, core_ref, *refs):
    ins, outs = refs[: len(plan)], list(refs[len(plan) :])
    for ref, (kind, groups, chips) in zip(ins, plan):
        if kind == "cast":
            outs.pop(0)[...] = ref[...].astype(HALF)
            continue
        size = ref.shape[1] // (groups * chips * 2)
        pick = lambda odd: jnp.concatenate(
            [ref[:, (2 * k + odd) * size : (2 * k + odd + 1) * size] for k in range(groups * chips)],
            axis=1,
        )
        even, odd = pick(0), pick(1)
        is_even = core_ref[0] == 0
        own = jnp.where(is_even, even, odd).astype(HALF)
        other = jnp.where(is_even, odd, even).astype(HALF)
        if kind == "split":
            outs.pop(0)[...] = own
            outs.pop(0)[...] = other
        else:
            out = outs.pop(0)
            out[:, : own.shape[1]] = own
            out[:, own.shape[1] :] = other


def split_call(name, core, weights, plan):
    outs = []
    for weight, (kind, _, _) in zip(weights, plan):
        size, columns = weight.shape
        if kind == "split":
            outs += [jax.ShapeDtypeStruct((size, columns // 2), HALF)] * 2
        else:
            outs.append(jax.ShapeDtypeStruct((size, columns), HALF))
    return pl.pallas_call(
        functools.partial(split_kernel, plan),
        in_specs=[pl.BlockSpec(memory_space=pltpu.SMEM)]
        + [pl.BlockSpec(memory_space=pltpu.VMEM)] * len(weights),
        out_specs=[pl.BlockSpec(memory_space=pltpu.VMEM)] * len(outs),
        out_shape=outs,
        compiler_params=pltpu.CompilerParams(vmem_limit_bytes=VMEM_BYTES),
        cost_estimate=cost(TAKES[name]),
        name=name,
    )(core, *weights)


def pack_kernel(width, split_count, chips, core_ref, *refs):
    *ins, out = refs
    at = 0
    for k in range(split_count):
        own, other = ins[2 * k], ins[2 * k + 1]
        rows = own.shape[0]
        is_even = core_ref[0] == 0
        for column in range(0, own.shape[1], width):
            mine, came = own[:, column : column + width], other[:, column : column + width]
            out[at : at + rows, :] = jnp.where(is_even, mine, came)
            out[at + rows : at + 2 * rows, :] = jnp.where(is_even, came, mine)
            at += 2 * rows
    for ref in ins[2 * split_count :]:
        rows, columns = ref.shape
        if chips and ref is ins[-1]:
            size = columns // (2 * chips)
            even, odd = (
                jnp.concatenate(
                    [ref[:, (2 * k + o) * size : (2 * k + o + 1) * size] for k in range(chips)],
                    axis=1,
                )
                for o in (0, 1)
            )
            is_even = core_ref[0] == 0
            whole = [jnp.where(is_even, even, odd), jnp.where(is_even, odd, even)]
            found = [v[:, c : c + width] for v in whole for c in range(0, columns // 2, width)]
        else:
            found = [ref[:, c : c + width] for c in range(0, columns, width)]
        for value in found:
            out[at : at + rows, :] = value.astype(HALF)
            at += rows


def pack_call(name, core, width, split, plain, chips=0):
    ins = [a for pair in split for a in pair] + list(plain)
    size = sum(a.size for a in ins) // width
    return pl.pallas_call(
        functools.partial(pack_kernel, width, len(split), chips),
        in_specs=[pl.BlockSpec(memory_space=pltpu.SMEM)]
        + [pl.BlockSpec(memory_space=pltpu.VMEM)] * len(ins),
        out_specs=pl.BlockSpec(memory_space=pltpu.VMEM),
        out_shape=jax.ShapeDtypeStruct((size, width), HALF),
        compiler_params=pltpu.CompilerParams(vmem_limit_bytes=VMEM_BYTES),
        cost_estimate=cost(TAKES[name]),
        name=name,
    )(core, *ins)


def condition_kernel(buckets, labels, times, classes, out, one, two, sems):
    count = out.shape[0]

    def copies(i):
        yield pltpu.make_async_copy(
            times.at[pl.ds(buckets[i], 1), :], one.at[pl.ds(i, 1), :], sems.at[0, i]
        )
        yield pltpu.make_async_copy(
            classes.at[pl.ds(labels[i], 1), :], two.at[pl.ds(i, 1), :], sems.at[1, i]
        )

    for i in range(count):
        for copy in copies(i):
            copy.start()
    for i in range(count):
        for copy in copies(i):
            copy.wait()
    out[...] = one[...] + two[...]


def condition_call(buckets, labels, times, classes):
    shape = (buckets.shape[0], times.shape[1])
    return pl.pallas_call(
        condition_kernel,
        in_specs=[pl.BlockSpec(memory_space=pltpu.SMEM)] * 2
        + [pl.BlockSpec(memory_space=pl.ANY)] * 2,
        out_specs=pl.BlockSpec(memory_space=pltpu.VMEM),
        out_shape=jax.ShapeDtypeStruct(shape, WIDE),
        scratch_shapes=[
            pltpu.VMEM(shape, WIDE),
            pltpu.VMEM(shape, WIDE),
            pltpu.SemaphoreType.DMA((2, shape[0])),
        ],
        cost_estimate=cost(TAKES["condition"]),
        name="condition",
    )(buckets, labels, times, classes)


def join_kernel(groups, chips, core_ref, own, other, out):
    size = own.shape[1] // (groups * chips)
    is_even = core_ref[0] == 0
    even = jnp.where(is_even, own[...], other[...]).astype(WIDE)
    odd = jnp.where(is_even, other[...], own[...]).astype(WIDE)
    parts = []
    for k in range(groups * chips):
        parts += [v[:, k * size : (k + 1) * size] for v in (even, odd)]
    out[...] = jnp.concatenate(parts, axis=1)


def join_call(name, core, own, other, groups, chips):
    rows, columns = own.shape
    return pl.pallas_call(
        functools.partial(join_kernel, groups, chips),
        in_specs=[pl.BlockSpec(memory_space=pltpu.SMEM)]
        + [pl.BlockSpec(memory_space=pltpu.VMEM)] * 2,
        out_specs=pl.BlockSpec(memory_space=pltpu.VMEM),
        out_shape=jax.ShapeDtypeStruct((rows, 2 * columns), WIDE),
        compiler_params=pltpu.CompilerParams(vmem_limit_bytes=VMEM_BYTES),
        cost_estimate=cost(4),
        name=name,
    )(core, own, other)


def last_kernel(value, *refs):
    refs[-1][...] = value[...]


def last_call(value, after):
    return pl.pallas_call(
        last_kernel,
        in_specs=[pl.BlockSpec(memory_space=pltpu.VMEM)]
        + [pl.BlockSpec(memory_space=pl.ANY)] * len(after),
        out_specs=pl.BlockSpec(memory_space=pltpu.VMEM),
        out_shape=jax.ShapeDtypeStruct(value.shape, value.dtype),
        cost_estimate=cost(1),
        name="last",
    )(value, *after)


def shards(
    n_dp,
    n_seq,
    image_tokens,
    cotangent,
    targets,
    bucket,
    labels,
    time_table,
    class_table,
    ada_weight,
    ada_bias,
    qkv_weight,
    qkv_bias,
    out_weight,
    out_bias,
    up_weight,
    up_bias,
    down_weight,
    down_bias,
    tap_first,
    tap_first_bias,
    tap_second,
    tap_second_bias,
    tap_third,
    tap_third_bias,
):
    images, part_rows, width = image_tokens.shape
    chips = n_dp // 2
    bits = chips.bit_length() - 1
    assert 1 << bits == chips and 2 * images == n_seq and n_seq & (n_seq - 1) == 0
    rows = 2 * images * part_rows
    place = lax.axis_index("dp")
    plane = lax.axis_index("seq")
    core, chip = place % 2, place // 2
    first_core = core == 0
    me = chip.astype(jnp.int32).reshape(1)

    def flip_core(array):
        return lax.ppermute(array, "dp", [(i, i ^ 1) for i in range(n_dp)])

    def flip_chip(array, bit):
        return lax.ppermute(array, "dp", [(i, i ^ (2 << bit)) for i in range(n_dp)])

    def flip_plane(array, bit):
        return lax.ppermute(array, "seq", [(i, i ^ (1 << bit)) for i in range(n_seq)])

    spent = []

    def later(array, *done):
        if not done:
            return array
        marks = []
        for item in done:
            item = DONE[item] if isinstance(item, str) else item
            marks.append(item)
        array, *marks = lax.optimization_barrier((array, *marks))
        spent.extend(marks)
        return array

    def pull(have, level, first):
        for r in range(chips):
            if r.bit_count() == level:
                bit = next(
                    b for b in ((first + k) % bits for k in range(bits)) if r >> b & 1
                )
                have[r] = flip_chip(have[r ^ 1 << bit], bit)

    def ranks(first):
        order = [(first + k) % bits for k in range(bits)]
        return sorted(range(chips), key=lambda r: [r >> b & 1 for b in order])

    def scatter_begin(arrays, plan, *done, under_way=()):
        found = []
        for k, (order, _, _) in enumerate(plan):
            first = next(f for f in range(bits) if ranks(f) == order)
            came = under_way[k] if under_way else flip_chip(arrays[2 * k + 1], first)
            found.append(([arrays[2 * k], later(came, *done)], first))
        sent = []
        for parts, first in found:
            for step in range(1, bits):
                half = parts[0].shape[0] // 2
                far = sum(p[half:].astype(WIDE) for p in parts).astype(HALF)
                came = flip_chip(far, (first + step) % bits)
                parts = [p[:half] for p in parts] + [came]
            sent.append(parts)
        return sent, [parts[1] for parts, _ in found]

    def scatter_end(sent, *done):
        found = [
            sum(p.astype(WIDE) for p in (*parts[:-1], later(parts[-1], *done))).astype(HALF)
            for parts in sent
        ]
        return found[0] if len(found) == 1 else jnp.concatenate(found)

    def halves(size):
        if size % 32:
            return [(ranks(0), 0, size)]
        return [(ranks(0), 0, size // 2), (ranks(1 % bits), size // 2, size // 2)]

    def sum_line(array, *windows):
        extra = n_seq // 4
        for bit in range(extra.bit_length() - 1):
            array = (array.astype(WIDE) + flip_plane(array, bit).astype(WIDE)).astype(HALF)

        def move(what, pairs):
            pairs = [(a * extra + k, b * extra + k) for a, b in pairs for k in range(extra)]
            return lax.ppermute(what, "seq", pairs)

        at = plane // extra
        half = array.shape[0] // 2
        came = later(move(array, [(0, 1), (3, 2)]), *windows)
        array = (array.astype(WIDE) + came.astype(WIDE)).astype(HALF)
        low, high = array[:half], array[half:]
        came = move(jnp.where(at == 1, high, low), [(1, 2), (2, 1)])
        kept = (jnp.where(at == 1, low, high).astype(WIDE) + came.astype(WIDE)).astype(HALF)
        came = move(kept, [(1, 2), (2, 1)])
        array = jnp.where(
            at == 1, jnp.concatenate([kept, came]), jnp.concatenate([came, kept])
        )
        came = move(array, [(1, 0), (2, 3)])
        return jnp.where((at == 1) | (at == 2), array, came)

    def sum_planes(array, seen=None, half_way=None):
        steps = range(n_seq.bit_length() - 1)
        for bit in steps:
            half = array.shape[0] // 2
            low, high = array[:half], array[half:]
            upper = (plane >> bit & 1) == 1
            came = flip_plane(jnp.where(upper, low, high), bit)
            if seen is not None:
                seen.append(came)
            array = (jnp.where(upper, high, low).astype(WIDE) + came.astype(WIDE)).astype(HALF)
        for bit in reversed(steps):
            if half_way is not None and bit == 0:
                array = later(array, half_way)
            came = flip_plane(array, bit)
            if seen is not None:
                seen.append(came)
            upper = (plane >> bit & 1) == 1
            array = jnp.where(
                upper, jnp.concatenate([came, array]), jnp.concatenate([array, came])
            )
        return array

    def routes(turn):
        pairs = []
        for at in range(n_dp):
            for z in range(n_seq):
                k = z ^ turn
                goal = (at - at % 2 + k // images, (at % 2) * images + k % images)
                pairs.append((at * n_seq + z, goal[0] * n_seq + goal[1]))
        return pairs

    def to_chip(array, depth, *after):
        half = array.shape[1] // 2
        found = []
        for turn in range(n_seq):
            k = plane ^ turn
            piece = lax.dynamic_slice(
                array, (k % images, (k // images) * half, 0), (1, half, array.shape[2])
            )[0]
            piece = later(piece, *([found[-depth]] if len(found) >= depth else []), *after)
            found.append(lax.ppermute(piece, ("dp", "seq"), routes(turn)))
        return found

    def from_chip(array, depth, windows=((),) * 4):
        half = array.shape[0] // n_seq
        found = []
        for turn in range(n_seq):
            back = [(b, a) for a, b in routes(turn)]
            piece = array[turn * half : (turn + 1) * half]
            piece = later(piece, *([found[-depth]] if len(found) >= depth else []))
            came = lax.ppermute(piece, ("dp", "seq"), back)
            found.append(later(came, *windows[turn % len(windows)]))
        pieces = list(found)
        stacked = jnp.stack(found)
        for bit in range(n_seq.bit_length() - 1):
            pairs = stacked.reshape(-1, 2, 1 << bit, *stacked.shape[1:])
            swapped = jnp.where((plane >> bit & 1) == 1, pairs[:, ::-1], pairs)
            stacked = swapped.reshape(stacked.shape)
        parts = stacked.reshape(2, images, half, array.shape[1])
        return parts.transpose(1, 0, 2, 3).reshape(images, 2 * half, array.shape[1]), pieces

    def by_core(array, groups):
        lead = array.shape[:-1]
        cut = array.reshape(*lead, groups, chips, 2, -1)
        even = cut[..., 0, :].reshape(*lead, -1)
        odd = cut[..., 1, :].reshape(*lead, -1)
        return jnp.where(first_core, even, odd), jnp.where(first_core, odd, even)

    def from_cores(own, other, groups):
        lead = own.shape[:-1]
        even = jnp.where(first_core, own, other).reshape(*lead, groups, chips, 1, -1)
        odd = jnp.where(first_core, other, own).reshape(*lead, groups, chips, 1, -1)
        return jnp.concatenate([even, odd], axis=-2).reshape(*lead, -1)

    def in_order(own, other):
        return jnp.where(
            first_core, jnp.concatenate([own, other]), jnp.concatenate([other, own])
        )

    def spread(array, columns):
        return jnp.concatenate(
            [array[:, k : k + columns] for k in range(0, array.shape[1], columns)]
        )

    def weight_of(groups, columns, height):
        if all(v % 16 == 0 for _, pieces in groups for p in pieces for v in (p[0], p[1], p[4], height)):
            arrays, found = [], []
            for places, pieces in groups:
                numbers = []
                for array, base in places:
                    known = [k for k, seen in enumerate(arrays) if seen is array]
                    numbers.append((known[0] if known else len(arrays), base))
                    if not known:
                        arrays.append(array)
                found.append((numbers, pieces))
            return arrays, (found, True, height, columns)
        blocks = []
        for r in range(chips):
            block = jnp.zeros((height, columns), HALF)
            for places, pieces in groups:
                array, base = places[r]
                for row, rows, column, wide, to_row, to_column in pieces:
                    part = array[base + row : base + row + rows, column : column + wide]
                    block = lax.dynamic_update_slice(block, part, (to_row, to_column))
            blocks.append(block)
        stacked = jnp.take(jnp.stack(blocks), jnp.arange(chips) ^ chip, axis=0)
        stacked = stacked.reshape(-1, columns)
        size = stacked.shape[0]
        return [stacked], ([([(0, 0)], [(0, size, 0, columns, 0, 0)])], False, size, columns)

    def stacked_weight(places, at, width, columns, height):
        pieces = [
            (at + k * height, height, 0, width, 0, k * width) for k in range(columns // width)
        ]
        return weight_of([(places, pieces)], columns, height)

    biases = (
        ada_bias,
        qkv_bias,
        out_bias,
        up_bias,
        down_bias,
        tap_first_bias,
        tap_second_bias,
        tap_third_bias,
    )
    core_at = core.astype(jnp.int32).reshape(1)
    qkv_own, qkv_other = split_call("split_qkv", core_at, [qkv_weight], [("split", 3, chips)])
    qkv_have = {0: in_order(qkv_own, flip_core(qkv_other))}
    pull(qkv_have, 1, 0)
    qkv_near = [qkv_have[1 << b] for b in range(bits)]
    def pull_rest(have, first):
        for level in range(2, bits + 1):
            pull(have, level, first)
        return [have[r] for r in range(chips) if r.bit_count() > 1]

    def pull_parts(have, split):
        places, came = [[None] * chips for _ in range(2)], []
        for k in range(2):
            part = {r: have[r][:split] if k == 0 else have[r][split:] for r in have}
            came.append(pull_rest(part, 1 - k))
            for r in range(chips):
                places[k][r] = (have[r], k * split) if r in have else (part[r], 0)
        return places, came

    qkv_height, qkv_columns = qkv_have[0].shape
    (low_places, high_places), (low_last, high_last) = pull_parts(qkv_have, qkv_height // 2)
    qkv_weights = weight_of(
        [
            (places, [(0, qkv_height // 2, 0, qkv_columns, at, 0)])
            for places, at in ((low_places, 0), (high_places, qkv_height // 2))
        ],
        qkv_columns,
        qkv_height,
    )
    qkv_rest = low_last + high_last
    packed = jnp.concatenate(biases).astype(HALF).astype(WIDE)
    packed = jnp.concatenate([packed, jnp.concatenate([bucket, labels]).astype(WIDE)])
    everyone = jnp.pad(packed, (0, -packed.shape[0] % 128)).reshape(1, -1)
    everyone = jnp.concatenate([everyone, flip_core(everyone)])
    for bit in range(bits):
        everyone = jnp.concatenate([everyone, flip_chip(everyone, bit)])
    everyone = jnp.concatenate(
        [
            lax.dynamic_slice(everyone, (place ^ d, 0), (1, everyone.shape[1]))
            for d in range(n_dp)
        ]
    )
    full, at = [], 0
    for bias in biases:
        full.append(everyone[:, at : at + bias.shape[0]].reshape(1, -1))
        at += bias.shape[0]
    bucket_all = everyone[:, at : at + images].reshape(-1).astype(jnp.int32)
    labels_all = everyone[:, at + images : at + 2 * images].reshape(-1).astype(jnp.int32)
    ada_bias_full, qkv_bias_full, out_bias_full, up_bias_full = full[:4]
    down_bias_full, first_bias_full, second_bias_full, third_bias_full = full[4:]
    qkv_bias_own = by_core(qkv_bias_full, 3)[0]
    up_bias_own = by_core(up_bias_full, 1)[0]
    first_bias_own = by_core(first_bias_full, 1)[0]
    second_bias_own = by_core(second_bias_full, 1)[0]

    up_weight = later(up_weight, qkv_have[0])
    up_own, up_other, first_own, first_other = split_call(
        "split_rest",
        core_at,
        [up_weight, tap_first],
        [("split", 1, chips), ("split", 1, chips)],
    )
    up_came, first_came = flip_core(up_other), flip_core(first_other)
    wide, narrow = width, math.gcd(tap_second.shape[1], tap_third.shape[1])
    near = pack_call(
        "pack_near", core_at, wide, [(up_own, up_came)], [down_weight, out_weight]
    )
    condition = condition_call(later(bucket_all, near, *qkv_near), labels_all, time_table, class_table)
    shard = ada_weight.shape[0]
    condition_own = lax.dynamic_slice(
        condition, (0, place * shard), (condition.shape[0], shard)
    )
    cond_act, cond_back = jax.vjp(jax.nn.silu, condition_own)
    cond_low = cond_act.astype(HALF)
    cond_plane = lax.dynamic_index_in_dim(
        cond_low.reshape(chips, n_seq, shard), plane, axis=1, keepdims=False
    )
    ada_low = ada_weight.astype(HALF)
    modulation = jnp.dot(cond_plane, ada_low, preferred_element_type=WIDE)
    modulation = later(modulation, *qkv_rest)
    modulation = modulation + flip_core(modulation)
    ranked = [
        lax.dynamic_slice(modulation, (chip ^ r, 0), (1, modulation.shape[1]))
        for r in range(chips)
    ]
    for bit in reversed(range(bits)):
        half = 1 << bit
        came = flip_chip(jnp.concatenate(ranked[half : 2 * half]), bit)
        ranked = [ranked[r] + came[r : r + 1] for r in range(half)]
    modulation = ranked[0] + ada_bias_full
    shift_one, scale_one, gate_one, shift_two, scale_two, gate_two = jnp.split(
        modulation, 6, axis=-1
    )

    same_core = [[2 * k + c for k in range(chips)] for c in range(2)]


    far = pack_call(
        "pack_far",
        core_at,
        narrow,
        [(first_own, first_came)],
        [tap_third, later(tap_second, qkv_have[1])],
        chips,
    )
    tokens_pieces = to_chip(image_tokens, 1)
    tokens_own = jnp.concatenate(tokens_pieces, axis=0)
    near_have = {0: later(near, modulation, *qkv_rest)}
    pull(near_have, 1, 0)
    near_own = [near_have[1 << b] for b in range(bits)]

    tile = 256 if rows % 512 == 0 else rows // 2
    heads = HEADS // 2
    tokens = jnp.concatenate([tokens_own, flip_core(tokens_own)])
    head_shape = (heads, rows, HEAD_DIM)
    inner = heads * HEAD_DIM
    hidden_ff = up_weight.shape[1] // 2
    tap_width = tap_first.shape[1] // 2
    tap_out = tap_third.shape[1]

    def flat(columns, dtype):
        return ((rows, columns), dtype, 0)

    def turned(columns):
        return ((columns, rows), HALF, 1)

    call = functools.partial(token_call, rows=rows, tile=tile)
    twice = functools.partial(token_call, rows=rows, tile=2 * tile)
    hidden_one_t, query, key, value = call(
        "qkv",
        qkv_body,
        me,
        [(tokens, False)],
        [shift_one, scale_one, qkv_bias_own],
        [qkv_weights],
        [turned(width)] + [(head_shape, HALF, 1)] * 3,
        [],
    )
    context, lse = attention_call(query, key, value)
    for r in [r for r in near_have if r]:
        near_have[r] = later(near_have[r], "attention")
    far_have = {0: far}
    height, high = 2 * up_own.shape[0], tap_second.shape[0]
    columns, tap_columns = up_own.shape[1], first_own.shape[1]
    cut = height * columns // wide
    (up_places, mixed_places), (up_last, _) = pull_parts(near_have, cut)
    up_weights = stacked_weight(up_places, 0, wide, columns, height)
    down_weights = stacked_weight(mixed_places, 0, wide, wide, down_weight.shape[0])
    out_weights = stacked_weight(
        mixed_places, down_weight.shape[0], wide, wide, out_weight.shape[0]
    )
    for bit in range(bits):
        far_have[1 << bit] = flip_chip(later(far, *near_own), bit)
    cut = height * tap_columns // narrow + high * tap_third.shape[1] // narrow
    (first_places, second_places), _ = pull_parts(far_have, cut)
    first_weights = stacked_weight(first_places, 0, narrow, tap_columns, height)
    third_weights = stacked_weight(
        first_places, height * tap_columns // narrow, narrow, tap_third.shape[1], high
    )
    second_weights = stacked_weight(second_places, 0, narrow, tap_second.shape[1], high)

    beside_pieces = to_chip(
        later(jnp.concatenate([cotangent, targets], axis=2), "qkv"), 1
    )
    beside = jnp.concatenate(beside_pieces)
    out_part, out_low, context_t = call(
        "out",
        out_body,
        me,
        [(context, False)],
        [],
        [out_weights],
        [flat(width, WIDE), flat(width, HALF), turned(inner)],
        [],
        after=[*up_last, far, beside_pieces[1]],
    )
    out_came = flip_core(out_low)
    mixed, hidden_two_t, upper, act_t, feed_part, feed_low = call(
        "feed",
        feed_body,
        me,
        [(tokens, False), (out_part, False), (out_came, True)],
        [gate_one, shift_two, scale_two, out_bias_full, up_bias_own],
        [up_weights, down_weights],
        [
            flat(width, WIDE),
            turned(width),
            flat(hidden_ff, WIDE),
            turned(hidden_ff),
            flat(width, WIDE),
            flat(width, HALF),
        ],
        [],
        after=[beside, *[far_have[1 << b] for b in range(bits)]],
    )
    feed_came = flip_core(feed_low)
    beside_all = jnp.concatenate([beside, flip_core(beside)])
    cotangent_all, targets_all = beside_all[:, :width], beside_all[:, width:]
    block_out, block_t, first_pre, first_t, second_part, second_low = call(
        "tap",
        tap_body,
        me,
        [(mixed, False), (feed_part, False), (feed_came, True)],
        [gate_two, down_bias_full, first_bias_own],
        [first_weights, second_weights],
        [
            flat(width, HALF),
            turned(width),
            flat(tap_width, WIDE),
            turned(tap_width),
            flat(tap_width, WIDE),
            flat(tap_width, HALF),
        ],
        [],
    )
    second_came = flip_core(second_low)
    second_pre, second_t, latent_part, latent_low = call(
        "latent",
        latent_body,
        me,
        [(second_part, False), (second_came, True)],
        [second_bias_own],
        [third_weights],
        [flat(tap_width, WIDE), turned(tap_width), flat(tap_out, WIDE), flat(tap_out, HALF)],
        [],
    )
    latent_came = flip_core(latent_low)

    dlatent, dsecond, cos_sum, third_bg, second_bg = call(
        "cosine",
        cosine_body,
        me,
        [(latent_part, False), (latent_came, True), (targets_all, False), (second_pre, False)],
        [third_bias_full],
        [third_weights],
        [flat(tap_out, HALF), flat(tap_width, HALF)],
        [(1, 128), (1, tap_out), (1, tap_width)],
    )
    dsecond_came = flip_core(dsecond)
    third_plan = [(ranks(1 % bits), 0, tap_third.shape[0])]
    third_wg = weight_grad_call("third_grad", me, second_t, [dlatent], third_plan, 384)
    second_plan = [(ranks(0), 0, tap_second.shape[0])]
    second_wg = weight_grad_call(
        "second_grad", me, first_t, [dsecond, dsecond_came], second_plan, 512, after=third_wg[:1]
    )
    dfirst, tap_part, tap_low, first_bg = call(
        "tap_back",
        tap_back_body,
        me,
        [(dsecond, False), (dsecond_came, True), (first_pre, False)],
        [],
        [second_weights, first_weights],
        [flat(tap_width, HALF), flat(width, WIDE), flat(width, HALF)],
        [(1, tap_width)],
        after=[second_wg[0]],
    )
    tap_came = flip_core(tap_low)
    block_output, block_pieces = from_chip(
        block_out[: rows // 2], 2, (("cosine",), ("cosine",), ("tap_back",), ("tap_back",))
    )
    third_sent, third_far = scatter_begin(third_wg, third_plan, "tap_back")
    first_plan = [(ranks(1 % bits), 0, height)]
    first_wg = weight_grad_call(
        "first_grad", me, block_t, [dfirst], first_plan, 512, after=third_far + block_pieces[:2]
    )
    doutput, dfeed, dupper, hidden_part, hidden_low, gate_two_grad, down_bg, up_bg = call(
        "feed_back",
        feed_back_body,
        me,
        [
            (cotangent_all, False),
            (tap_part, False),
            (tap_came, True),
            (feed_part, False),
            (feed_came, True),
            (upper, False),
        ],
        [gate_two, down_bias_full],
        [down_weights, up_weights],
        [
            flat(width, WIDE),
            flat(width, HALF),
            flat(hidden_ff, HALF),
            flat(width, WIDE),
            flat(width, HALF),
        ],
        [(1, width), (1, width), (1, hidden_ff)],
        after=[first_wg[0], *block_pieces],
    )

    first_sent, first_far = scatter_begin(first_wg, first_plan, "feed_back")
    third_part = lax.psum(scatter_end(third_sent, "first_grad"), "seq")
    hidden_came = flip_core(hidden_low)
    down_plan = halves(down_weight.shape[0])
    down_wg = weight_grad_call(
        "down_grad", me, act_t, [dfeed], down_plan, 256, after=[*first_far, third_part]
    )
    second_sent, second_far = scatter_begin(second_wg, second_plan, "down_grad")
    up_plan = halves(height)
    up_wg = weight_grad_call(
        "up_grad", me, hidden_two_t, [dupper], up_plan, 768, after=[down_wg[0], *second_far]
    )
    first_sum = scatter_end(first_sent, "down_grad")
    first_sum = lax.psum(later(first_sum, third_part), "seq")
    (
        dmixed,
        dattended,
        dcontext,
        shift_two_grad,
        scale_two_grad,
        gate_one_grad,
        out_bg,
    ) = call(
        "mix_back",
        mix_back_body,
        me,
        [
            (mixed, False),
            (doutput, False),
            (hidden_part, False),
            (hidden_came, True),
            (out_part, False),
            (out_came, True),
        ],
        [scale_two, gate_one, out_bias_full],
        [out_weights],
        [flat(width, WIDE), flat(width, HALF), (head_shape, HALF, 1)],
        [(1, width)] * 4,
        after=[up_wg[0]],
    )
    down_sent, down_far = scatter_begin(down_wg, down_plan, "mix_back")
    out_plan = [(ranks(0), 0, out_weight.shape[0])]
    out_wg = weight_grad_call(
        "out_grad", me, context_t, [dattended], out_plan, 384
    )
    dquery, dkey, dvalue = attention_back_call(
        query, key, value, dcontext, lse, after=[out_wg[0], first_sum, *[parts[-1] for parts in down_sent]]
    )
    second_sum = scatter_end(second_sent, "mix_back")
    second_sum = lax.psum(later(second_sum, first_sum), "seq")
    up_under_way = [
        flip_chip(later(up_wg[2 * k + 1], *down_far), k) for k in range(len(up_plan))
    ]
    up_sent, up_far = scatter_begin(
        up_wg, up_plan, "attention_back", under_way=up_under_way
    )
    dqkv, one_part, one_low, qkv_bg = call(
        "qkv_back",
        qkv_back_body,
        me,
        [(dquery, False), (dkey, False), (dvalue, False)],
        [],
        [qkv_weights],
        [flat(3 * inner, HALF), flat(width, WIDE), flat(width, HALF)],
        [(1, 3 * inner)],
        after=[second_sum, *up_far],
    )
    one_came = flip_core(one_low[rows // 2 :])
    qkv_plan = halves(qkv_have[0].shape[0])
    out_sent, out_far = scatter_begin(out_wg, out_plan, "qkv_back")
    qkv_wg = weight_grad_call(
        "qkv_grad", me, hidden_one_t, [dqkv], qkv_plan, 256
    )
    up_part = scatter_end(up_sent, "qkv_grad")
    out_part = scatter_end(out_sent, "qkv_grad")
    down_part = scatter_end(down_sent, "attention_back")
    down_part = lax.psum(later(down_part, second_sum), "seq")
    up_part = lax.psum(later(up_part, down_part), "seq")
    input_low, shift_one_grad, scale_one_grad = token_call(
        "input_grad",
        input_body,
        me,
        [(tokens, False), (dmixed, False), (one_part, False), (one_came, False)],
        [scale_one],
        [],
        [((rows // 2, width), HALF, 0)],
        [(1, width)] * 2,
        rows=rows // 2,
        tile=tile,
        after=[qkv_wg[0], down_part, *out_far],
    )
    input_grad = from_chip(input_low, 2)[0].astype(WIDE)

    qkv_sent, qkv_far = scatter_begin(qkv_wg, qkv_plan, "input_grad")
    qkv_scattered = scatter_end(qkv_sent)
    qkv_part, out_part = lax.psum((later(qkv_scattered, up_part), out_part), "seq")
    qkv_hops = [qkv_scattered, qkv_scattered]
    one_grads = jnp.concatenate([shift_one_grad, scale_one_grad], axis=1)
    one_grads = later(one_grads + flip_core(one_grads), *qkv_far)
    modulation_grad = jnp.concatenate(
        [one_grads, gate_one_grad, shift_two_grad, scale_two_grad, gate_two_grad], axis=1
    )
    for bit in range(bits):
        modulation_grad = jnp.concatenate([modulation_grad, flip_chip(modulation_grad, bit)])
    modulation_grad = later(modulation_grad, up_part)
    for bit in range(n_seq.bit_length() - 1):
        modulation_grad = jnp.concatenate([modulation_grad, flip_plane(modulation_grad, bit)])
    nth = jnp.arange(chips * n_seq)
    picked = ((nth % chips) ^ chip) * n_seq + ((nth // chips) ^ plane)
    pick = (picked[:, None] == jnp.arange(chips * n_seq)[None, :]).astype(WIDE)
    modulation_all = later(jnp.dot(pick.T, modulation_grad, precision=HIGH), qkv_hops[-1])
    ada_wg = jnp.einsum(
        "bi,bj->ij", cond_low.astype(WIDE), modulation_all, precision=HIGH
    )
    ada_size = ada_bias.shape[0]
    ada_bg = lax.dynamic_slice(jnp.sum(modulation_all, axis=0), (place * ada_size,), (ada_size,))
    cond_grad = cond_back(
        jnp.einsum("bj,ij->bi", modulation_all, ada_low.astype(WIDE), precision=HIGH)
    )[0]
    cond_grad = lax.all_gather(cond_grad, "dp", axis=1, tiled=True)
    time_hot = (
        bucket_all[:, None] == jnp.arange(time_table.shape[0], dtype=jnp.int32)[None, :]
    ).astype(WIDE)
    class_hot = (
        labels_all[:, None] == jnp.arange(class_table.shape[0], dtype=jnp.int32)[None, :]
    ).astype(WIDE)
    time_grad = jnp.einsum("bt,bd->td", time_hot, cond_grad, precision=HIGH)
    class_grad = jnp.einsum("bt,bd->td", class_hot, cond_grad, precision=HIGH)

    sums = [qkv_bg, up_bg, first_bg, second_bg, out_bg, down_bg, third_bg, cos_sum]
    line = later(jnp.concatenate(sums, axis=1), qkv_scattered)
    for bit in range(bits):
        line = line + flip_chip(line, bit)
    for bit in range(n_seq.bit_length() - 1):
        line = line + flip_plane(line, bit)
    line = later(line, qkv_hops[0])
    split_at = sum(s.shape[1] for s in sums[:4])
    came = flip_core(line[:, :split_at])
    bias_grads, at = [], 0
    for k, (item, groups) in enumerate(zip(sums[:4], (3, 1, 1, 1))):
        size = item.shape[1]
        bias_grads.append(
            from_cores(line[:, at : at + size], came[:, at : at + size], groups)
        )
        at += size
    for item in sums[4:7]:
        bias_grads.append(line[:, at : at + item.shape[1]])
        at += item.shape[1]
    align_loss = -0.5 * line[:, at : at + 1] / (rows * chips * n_seq)

    def own_part(grad):
        size = grad.shape[1] // n_dp
        return lax.dynamic_slice(grad, (0, place * size), (1, size))[0]

    qkv_bo, up_bo, first_bo, second_bo, out_bo, down_bo, third_bo = map(own_part, bias_grads)

    def whole_columns(grad, groups):
        size = grad.shape[0] // 2
        own = lax.dynamic_slice(grad, (core * size, 0), (size, grad.shape[1]))
        other = lax.dynamic_slice(grad, ((1 - core) * size, 0), (size, grad.shape[1]))
        return join_call("join", core_at, own, flip_core(other), groups, chips)

    block_output = later(block_output, "input_grad")
    third_part, second_sum, first_sum, down_part, up_part, out_part = (
        later(a, "input_grad", qkv_scattered)
        for a in (third_part, second_sum, first_sum, down_part, up_part, out_part)
    )
    third_own = third_part.astype(WIDE)
    second_own = join_call(
        "join", core_at, second_sum[:, :tap_width], second_sum[:, tap_width:], 1, chips
    )
    first_own = whole_columns(first_sum, 1)
    down_own = down_part.astype(WIDE)
    up_own = whole_columns(up_part, 1)
    out_own = out_part.astype(WIDE)
    qkv_own = whole_columns(qkv_part, 3)
    align_loss = last_call(align_loss, spent)[0, 0]
    return (
        block_output,
        input_grad,
        align_loss,
        time_grad,
        class_grad,
        ada_wg,
        ada_bg,
        qkv_own,
        qkv_bo,
        out_own,
        out_bo,
        up_own,
        up_bo,
        down_own,
        down_bo,
        first_own,
        first_bo,
        second_own,
        second_bo,
        third_own,
        third_bo,
    )


def solution(mesh):
    tokens, rows, line = P("dp", "seq", None), P("dp", None), P("dp")
    return jax.shard_map(
        functools.partial(shards, mesh.shape["dp"], mesh.shape["seq"]),
        mesh=mesh,
        in_specs=(tokens, tokens, tokens, line, line, P(), P()) + (rows, line) * 8,
        out_specs=(tokens, tokens, P(), P(), P()) + (rows, line) * 8,
        check_vma=False,
    )
```

```python
import functools
import math

import jax
import jax.numpy as jnp
from jax import lax
from jax.experimental import pallas as pl
from jax.experimental.pallas import tpu as pltpu
from jax.sharding import PartitionSpec as P

HEADS = 16
HEAD_DIM = 72
EPS_NORM = 1e-06
HIGH = lax.Precision.HIGHEST
HALF = jnp.bfloat16
WIDE = jnp.float32
VMEM_BYTES = 56 * 1024 * 1024
GELU_A = math.sqrt(2.0 / math.pi)
GELU_B = 0.044715
SCALE = 1
MARK = (8, 128)
DONE = {}
TAKES = {
    "qkv": 13,
    "attention": 30,
    "out": 8,
    "feed": 27,
    "tap": 16,
    "latent": 9,
    "cosine": 9,
    "tap_back": 16,
    "third_grad": 5,
    "second_grad": 8,
    "first_grad": 6,
    "feed_back": 28,
    "down_grad": 12,
    "up_grad": 12,
    "mix_back": 14,
    "out_grad": 5,
    "attention_back": 31,
    "qkv_back": 12,
    "qkv_grad": 10,
    "input_grad": 5,
    "split_qkv": 3,
    "split_rest": 3,
    "pack_near": 4,
    "pack_far": 4,
    "condition": 2,
}


def cost(microseconds):
    return pl.CostEstimate(
        flops=int(microseconds * SCALE * 1.15e9),
        bytes_accessed=int(microseconds * SCALE * 3.6e6),
        transcendentals=0,
    )


def dot(left, right):
    return jnp.dot(left, right, preferred_element_type=WIDE)


def dot_nt(left, right):
    return lax.dot_general(left, right, (((1,), (1,)), ((), ())), preferred_element_type=WIDE)


def normed(values):
    centre = values - jnp.mean(values, axis=-1, keepdims=True)
    spread = jnp.mean(centre * centre, axis=-1, keepdims=True)
    inverse = lax.rsqrt(spread + EPS_NORM)
    return centre * inverse, inverse


def normed_back(norm, inverse, grad):
    return (
        grad
        - jnp.mean(grad, axis=-1, keepdims=True)
        - norm * jnp.mean(grad * norm, axis=-1, keepdims=True)
    ) * inverse


def sigmoid(values):
    return 1.0 / (1.0 + jnp.exp(-values))


def silu_back(pre, grad):
    gate = sigmoid(pre)
    return grad * (gate * (1.0 + pre * (1.0 - gate)))


def gelu(values):
    inner = jnp.tanh(GELU_A * (values + GELU_B * (values * values * values)))
    return 0.5 * values * (1.0 + inner)


def gelu_back(values, grad):
    square = values * values
    inner = jnp.tanh(GELU_A * (values + GELU_B * (square * values)))
    slope = 0.5 * (1.0 + inner) + 0.5 * values * (1.0 - inner * inner) * (
        GELU_A * (1.0 + 3.0 * GELU_B * square)
    )
    return grad * slope


def total(values):
    return jnp.sum(values, axis=0, keepdims=True)


def spans(size, most):
    count = -(-size // most)
    while size % count or (size // count) % 128:
        count += 1
        if count > size // 128:
            return [(0, size)]
    return [(k * (size // count), size // count) for k in range(count)]


def joined(ref, index=slice(None)):
    return jnp.concatenate([ref[h] for h in range(ref.shape[0])], axis=-1)


class Weight:
    def __init__(self, me, step, arrays, how, store, sems):
        self.me, self.step, self.arrays, self.how = me, step, arrays, how
        self.store, self.sems = store, sems

    def copies(self):
        groups, by_me, height, _ = self.how
        count = 0
        for places, pieces in groups:
            for r, (number, base) in enumerate(places):
                start = pl.multiple_of((self.me ^ r) * height, height) if by_me else r * height
                for row, rows, column, columns, to_row, to_column in pieces:
                    yield pltpu.make_async_copy(
                        self.arrays[number].at[pl.ds(base + row, rows), pl.ds(column, columns)],
                        self.store.at[pl.ds(start + to_row, rows), pl.ds(to_column, columns)],
                        self.sems.at[count],
                    )
                    count += 1

    def start(self):
        @pl.when(self.step == 0)
        def _():
            for copy in self.copies():
                copy.start()

    def ready(self):
        @pl.when(self.step == 0)
        def _():
            for copy in self.copies():
                copy.wait()

        return self.store


def token_kernel(body, counts, hows, me_ref, *refs):
    n_tok, n_const, n_blocks, n_after, n_out, n_sum = counts
    refs = list(refs)
    take = lambda n: [refs.pop(0) for _ in range(n)]
    toks, consts = take(n_tok), take(n_const)
    blocks = [take(n) for n in n_blocks]
    take(n_after)
    outs, sums, (mark,) = take(n_out), take(n_sum), take(1)
    step = pl.program_id(0)

    @pl.when(step == 0)
    def _():
        mark[...] = jnp.zeros_like(mark)

    weights = [
        Weight(me_ref[0], step, group, hows[k], refs[2 * k], refs[2 * k + 1])
        for k, group in enumerate(blocks)
    ]
    for weight in weights:
        weight.start()
    if sums:

        @pl.when(step == 0)
        def _():
            for ref in sums:
                ref[...] = jnp.zeros_like(ref)

    body(toks, consts, weights, outs, sums)


def token_call(name, body, me, toks, consts, weights, outs, sums, rows, tile, after=()):
    steps = rows // tile

    def spec(shape, dim, swapped=False):
        block = tuple(tile if k == dim else s for k, s in enumerate(shape))

        def place(i, me_ref):
            at = lax.rem(i + steps // 2, steps) if swapped else i
            return tuple(at if k == dim else 0 for k in range(len(shape)))

        return pl.BlockSpec(block, place)

    def whole(shape):
        return pl.BlockSpec(shape, lambda i, me_ref: (0,) * len(shape))

    in_specs = [spec(a.shape, a.ndim - 2, swapped) for a, swapped in toks]
    in_specs += [whole(c.shape) for c in consts]
    blocks = [array for group, _ in weights for array in group]
    in_specs += [pl.BlockSpec(memory_space=pl.ANY)] * (len(blocks) + len(after))
    out_specs = [spec(shape, dim) for shape, _, dim in outs] + [whole(shape) for shape in sums]
    out_shape = [jax.ShapeDtypeStruct(shape, dtype) for shape, dtype, _ in outs]
    out_shape += [jax.ShapeDtypeStruct(shape, WIDE) for shape in sums]
    out_specs.append(whole(MARK))
    out_shape.append(jax.ShapeDtypeStruct(MARK, WIDE))
    scratch = []
    for _, (groups, _, height, columns) in weights:
        scratch += [
            pltpu.VMEM((height * len(groups[0][0]), columns), HALF),
            pltpu.SemaphoreType.DMA((sum(len(a) * len(b) for a, b in groups),)),
        ]
    counts = (len(toks), len(consts), [len(g) for g, _ in weights], len(after), len(outs), len(sums))
    *found, DONE[name] = pl.pallas_call(
        functools.partial(token_kernel, body, counts, [how for _, how in weights]),
        grid_spec=pltpu.PrefetchScalarGridSpec(
            num_scalar_prefetch=1,
            grid=(steps,),
            in_specs=in_specs,
            out_specs=out_specs,
            scratch_shapes=scratch,
        ),
        out_shape=out_shape,
        compiler_params=pltpu.CompilerParams(
            dimension_semantics=("arbitrary",), vmem_limit_bytes=VMEM_BYTES
        ),
        cost_estimate=cost(TAKES[name]),
        name=name,
    )(me, *[a for a, _ in toks], *consts, *blocks, *after)
    return found


def qkv_body(toks, consts, weights, outs, sums):
    (x,), (shift, scale, bias), (weight,) = toks, consts, weights
    hidden_t, query, key, value = outs
    norm, _ = normed(x[...].astype(WIDE))
    hidden = norm * (1.0 + scale[...]) + shift[...]
    low = hidden.astype(HALF)
    hidden_t[...] = hidden.T.astype(HALF)
    store = weight.ready()
    width = store.shape[1] // 3
    for k, out in enumerate((query, key, value)):
        part = dot(low, store[:, k * width : (k + 1) * width])
        part = (part + bias[:, k * width : (k + 1) * width]).astype(HALF)
        for h in range(out.shape[0]):
            out[h] = part[:, h * HEAD_DIM : (h + 1) * HEAD_DIM]


def attention_kernel(query, key, value, *refs):
    context, lse, mark = refs[-3:]
    mark[...] = jnp.zeros_like(mark)
    factor = 1.0 / math.sqrt(HEAD_DIM)
    keys, values = key[0], value[0]
    rows = query.shape[1]
    tile = min(rows, 256)
    for start in range(0, rows, tile):
        at = slice(start, start + tile)
        scores = dot_nt(keys, query[0, at, :]) * factor
        highest = jnp.max(scores, axis=0, keepdims=True)
        expo = jnp.exp(scores - highest)
        summed = jnp.sum(expo, axis=0, keepdims=True)
        probs = (expo / summed).astype(HALF)
        lse[0, :, at] = highest + jnp.log(summed)
        found = lax.dot_general(
            values, probs, (((0,), (0,)), ((), ())), preferred_element_type=WIDE
        )
        context[0, at, :] = found.T.astype(HALF)


def attention_call(query, key, value, after=()):
    heads, rows, _ = query.shape
    block = pl.BlockSpec((1, rows, HEAD_DIM), lambda h: (h, 0, 0))
    line = pl.BlockSpec((1, 1, rows), lambda h: (h, 0, 0))
    *found, DONE["attention"] = pl.pallas_call(
        attention_kernel,
        grid=(heads,),
        in_specs=[block] * 3 + [pl.BlockSpec(memory_space=pl.ANY)] * len(after),
        out_specs=[block, line, pl.BlockSpec(MARK, lambda h: (0, 0))],
        out_shape=[
            jax.ShapeDtypeStruct(query.shape, HALF),
            jax.ShapeDtypeStruct((heads, 1, rows), WIDE),
            jax.ShapeDtypeStruct(MARK, WIDE),
        ],
        compiler_params=pltpu.CompilerParams(
            dimension_semantics=("arbitrary",), vmem_limit_bytes=VMEM_BYTES
        ),
        cost_estimate=cost(TAKES["attention"]),
        name="attention",
    )(query, key, value, *after)
    return found


def attention_back_kernel(query, key, value, grad, lse, *refs):
    dquery, dkey, dvalue, mark, sum_key, sum_value = refs[-6:]
    mark[...] = jnp.zeros_like(mark)
    factor = 1.0 / math.sqrt(HEAD_DIM)
    keys, values = key[0], value[0]
    rows = query.shape[1]
    tile = min(rows, 256)
    for start in range(0, rows, tile):
        at = slice(start, start + tile)
        queries, grads = query[0, at, :], grad[0, at, :]
        probs = jnp.exp(dot_nt(keys, queries) * factor - lse[0, :, at])
        dprobs = dot_nt(values, grads)
        held = jnp.sum(probs * dprobs, axis=0, keepdims=True)
        dscores = (probs * (dprobs - held)).astype(HALF)
        value_part = dot(probs.astype(HALF), grads)
        key_part = dot(dscores, queries)
        if start == 0:
            sum_value[...] = value_part
            sum_key[...] = key_part
        else:
            sum_value[...] += value_part
            sum_key[...] += key_part
        found = lax.dot_general(
            keys, dscores, (((0,), (0,)), ((), ())), preferred_element_type=WIDE
        )
        dquery[0, at, :] = (found * factor).T.astype(HALF)
    dkey[0] = (sum_key[...] * factor).astype(HALF)
    dvalue[0] = sum_value[...].astype(HALF)


def attention_back_call(query, key, value, grad, lse, after=()):
    heads, rows, _ = query.shape
    block = pl.BlockSpec((1, rows, HEAD_DIM), lambda h: (h, 0, 0))
    line = pl.BlockSpec((1, 1, rows), lambda h: (h, 0, 0))
    *found, DONE["attention_back"] = pl.pallas_call(
        attention_back_kernel,
        grid=(heads,),
        in_specs=[block] * 4 + [line] + [pl.BlockSpec(memory_space=pl.ANY)] * len(after),
        out_specs=[block] * 3 + [pl.BlockSpec(MARK, lambda h: (0, 0))],
        out_shape=[jax.ShapeDtypeStruct(query.shape, HALF)] * 3
        + [jax.ShapeDtypeStruct(MARK, WIDE)],
        scratch_shapes=[pltpu.VMEM((rows, HEAD_DIM), WIDE)] * 2,
        compiler_params=pltpu.CompilerParams(
            dimension_semantics=("arbitrary",), vmem_limit_bytes=VMEM_BYTES
        ),
        cost_estimate=cost(TAKES["attention_back"]),
        name="attention_back",
    )(query, key, value, grad, lse, *after)
    return found


def out_body(toks, consts, weights, outs, sums):
    (context,), (weight,) = toks, weights
    part, low, context_t = outs
    heads = joined(context)
    context_t[...] = heads.astype(WIDE).T.astype(HALF)
    found = dot(heads, weight.ready()[...])
    part[...] = found
    low[...] = found.astype(HALF)


def feed_body(toks, consts, weights, outs, sums):
    x, part, other = toks
    gate_one, shift, scale, out_bias, up_bias = consts
    up, down = weights
    mixed, hidden_t, upper, act_t, feed, feed_low = outs
    attended = part[...] + other[...].astype(WIDE) + out_bias[...]
    mix = x[...].astype(WIDE) + gate_one[...] * attended
    mixed[...] = mix
    norm, _ = normed(mix)
    hidden = norm * (1.0 + scale[...]) + shift[...]
    low = hidden.astype(HALF)
    hidden_t[...] = hidden.T.astype(HALF)
    up_store = up.ready()
    acc = None
    for k, (start, size) in enumerate(spans(up_store.shape[1], 768)):
        at = slice(start, start + size)
        pre = dot(low, up_store[:, at]) + up_bias[:, at]
        upper[:, at] = pre
        act = gelu(pre)
        act_t[at, :] = act.T.astype(HALF)
        if k == 0:
            down_store = down.ready()
        term = dot(act.astype(HALF), down_store[at, :])
        acc = term if acc is None else acc + term
    feed[...] = acc
    feed_low[...] = acc.astype(HALF)


def tap_body(toks, consts, weights, outs, sums):
    mixed, part, other = toks
    gate_two, down_bias, first_bias = consts
    first, second = weights
    block_out, block_t, first_pre, first_t, own, sent = outs
    feed = part[...] + other[...].astype(WIDE) + down_bias[...]
    output = mixed[...] + gate_two[...] * feed
    low = output.astype(HALF)
    block_out[...] = low
    block_t[...] = output.T.astype(HALF)
    pre = dot(low, first.ready()[...]) + first_bias[...]
    first_pre[...] = pre
    act = pre * sigmoid(pre)
    first_t[...] = act.T.astype(HALF)
    act_low = act.astype(HALF)
    store = second.ready()
    half = store.shape[1] // 2
    own[...] = dot(act_low, store[:, :half])
    sent[...] = dot(act_low, store[:, half:]).astype(HALF)


def latent_body(toks, consts, weights, outs, sums):
    (part, other), (bias,), (third,) = toks, consts, weights
    second_pre, second_t, own, low = outs
    pre = part[...] + other[...].astype(WIDE) + bias[...]
    second_pre[...] = pre
    act = pre * sigmoid(pre)
    second_t[...] = act.T.astype(HALF)
    found = dot(act.astype(HALF), third.ready()[...])
    own[...] = found
    low[...] = found.astype(HALF)


def cosine_body(toks, consts, weights, outs, sums):
    part, other, targets, second_pre = toks
    (bias,), (third,) = consts, weights
    dlatent, dsecond = outs
    cos_sum, third_bias_sum, second_bias_sum = sums
    latent = part[...] + other[...].astype(WIDE) + bias[...]
    target = targets[...].astype(WIDE)
    inner = jnp.sum(latent * target, axis=-1, keepdims=True)
    length = jnp.sum(latent * latent, axis=-1, keepdims=True) + EPS_NORM
    inverse = lax.rsqrt(length)
    inverse_target = lax.rsqrt(jnp.sum(target * target, axis=-1, keepdims=True) + EPS_NORM)
    cos = inner * inverse * inverse_target
    cos_sum[...] += jnp.broadcast_to(total(cos), cos_sum.shape)
    low = (-0.5 * (target * (inverse * inverse_target) - latent * (cos / length))).astype(HALF)
    dlatent[...] = low
    third_bias_sum[...] += total(low.astype(WIDE))
    pre_grad = silu_back(second_pre[...], dot_nt(low, third.ready()[...])).astype(HALF)
    dsecond[...] = pre_grad
    second_bias_sum[...] += total(pre_grad.astype(WIDE))


def tap_back_body(toks, consts, weights, outs, sums):
    own, other, first_pre = toks
    second, first = weights
    dfirst, part, low = outs
    (bias_sum,) = sums
    grads = jnp.concatenate([own[...], other[...]], axis=-1)
    pre_grad = silu_back(first_pre[...], dot_nt(grads, second.ready()[...])).astype(HALF)
    dfirst[...] = pre_grad
    bias_sum[...] += total(pre_grad.astype(WIDE))
    found = dot_nt(pre_grad, first.ready()[...])
    part[...] = found
    low[...] = found.astype(HALF)


def feed_back_body(toks, consts, weights, outs, sums):
    cotangent, part, other, feed_part, feed_other, upper = toks
    gate_two, down_bias = consts
    down, up = weights
    doutput, dfeed, dupper, hidden, hidden_low = outs
    gate_sum, down_bias_sum, up_bias_sum = sums
    grad = cotangent[...].astype(WIDE) + part[...] + other[...].astype(WIDE)
    doutput[...] = grad
    feed = feed_part[...] + feed_other[...].astype(WIDE) + down_bias[...]
    gate_sum[...] += total(grad * feed)
    low = (grad * gate_two[...]).astype(HALF)
    dfeed[...] = low
    down_bias_sum[...] += total(low.astype(WIDE))
    down_store = down.ready()
    acc = None
    for k, (start, size) in enumerate(spans(down_store.shape[0], 768)):
        at = slice(start, start + size)
        pre_grad = gelu_back(upper[:, at], dot_nt(low, down_store[at, :])).astype(HALF)
        dupper[:, at] = pre_grad
        up_bias_sum[:, at] += total(pre_grad.astype(WIDE))
        if k == 0:
            up_store = up.ready()
        term = dot_nt(pre_grad, up_store[:, at])
        acc = term if acc is None else acc + term
    hidden[...] = acc
    hidden_low[...] = acc.astype(HALF)


def mix_back_body(toks, consts, weights, outs, sums):
    mixed, doutput, part, other, out_part, out_other = toks
    scale, gate_one, out_bias = consts
    (weight,) = weights
    dmixed, dattended, dcontext = outs
    shift_sum, scale_sum, gate_sum, bias_sum = sums
    grad = part[...] + other[...].astype(WIDE)
    norm, inverse = normed(mixed[...])
    shift_sum[...] += total(grad)
    scale_sum[...] += total(grad * norm)
    mix_grad = doutput[...] + normed_back(norm, inverse, grad * (1.0 + scale[...]))
    dmixed[...] = mix_grad
    attended = out_part[...] + out_other[...].astype(WIDE) + out_bias[...]
    gate_sum[...] += total(mix_grad * attended)
    low = (mix_grad * gate_one[...]).astype(HALF)
    dattended[...] = low
    bias_sum[...] += total(low.astype(WIDE))
    found = dot_nt(low, weight.ready()[...]).astype(HALF)
    for h in range(dcontext.shape[0]):
        dcontext[h] = found[:, h * HEAD_DIM : (h + 1) * HEAD_DIM]


def qkv_back_body(toks, consts, weights, outs, sums):
    (weight,) = weights
    grads, part, low = outs
    (bias_sum,) = sums
    row = jnp.concatenate([joined(ref) for ref in toks], axis=-1)
    grads[...] = row
    bias_sum[...] += total(row.astype(WIDE))
    found = dot_nt(row, weight.ready()[...])
    part[...] = found
    low[...] = found.astype(HALF)


def input_body(toks, consts, weights, outs, sums):
    x, dmixed, part, other = toks
    (scale,) = consts
    (found,) = outs
    shift_sum, scale_sum = sums
    grad = part[...] + other[...].astype(WIDE)
    norm, inverse = normed(x[...].astype(WIDE))
    shift_sum[...] += total(grad)
    scale_sum[...] += total(grad * norm)
    result = dmixed[...] + normed_back(norm, inverse, grad * (1.0 + scale[...]))
    found[...] = result.astype(HALF)


def weight_grad_kernel(plan, size, sides, me_ref, left, *refs):
    count = 2 * len(plan)
    rights, (*outs, mark, hold) = refs[:sides], refs[-2 - count :]
    mark[...] = jnp.zeros_like(mark)

    def emit(found):
        hold[...] = found.astype(hold.dtype)
        for (ranks, row, rows), near, far in zip(plan, outs[::2], outs[1::2]):
            for k, r in enumerate(ranks):
                start = pl.multiple_of((me_ref[0] ^ r) * size + row, math.gcd(size, row or size))
                out = near if k < len(ranks) // 2 else far
                at = k % (len(ranks) // 2) * rows
                out[at : at + rows, :] = hold[pl.ds(start, rows), :].astype(HALF)

    if sides == 1:
        emit(dot(left[...], rights[0][...]))
        return
    is_own = pl.program_id(0) < pl.num_programs(0) // 2

    @pl.when(is_own)
    def _():
        emit(dot(left[...], rights[0][...]))

    @pl.when(jnp.logical_not(is_own))
    def _():
        half = left.shape[1] // 2
        emit(
            dot(left[:, :half], rights[1][half:, :]) + dot(left[:, half:], rights[1][:half, :])
        )


def weight_grad_call(name, me, left, rights, plan, tile, after=()):
    features, rows = left.shape
    columns = rights[0].shape[1]
    sides = len(rights)
    size = features // len(plan[0][0])
    tile = min(tile, columns)
    steps = pl.cdiv(columns, tile)
    hold = HALF if all(row % 16 == 0 and part % 16 == 0 for _, row, part in plan) else WIDE
    assert sides == 1 or columns % tile == 0
    outs = [(part * len(ranks) // 2, sides * columns) for ranks, _, part in plan for _ in range(2)]
    *found, DONE[name] = pl.pallas_call(
        functools.partial(weight_grad_kernel, plan, size, sides),
        grid_spec=pltpu.PrefetchScalarGridSpec(
            num_scalar_prefetch=1,
            grid=(sides * steps,),
            in_specs=[
                pl.BlockSpec((features, rows), lambda n, me_ref: (0, 0)),
                pl.BlockSpec((rows, tile), lambda n, me_ref: (0, jnp.minimum(n, steps - 1))),
                pl.BlockSpec((rows, tile), lambda n, me_ref: (0, jnp.maximum(n - steps, 0))),
            ][: 1 + sides]
            + [pl.BlockSpec(memory_space=pl.ANY)] * len(after),
            out_specs=[pl.BlockSpec((o[0], tile), lambda n, me_ref: (0, n)) for o in outs]
            + [pl.BlockSpec(MARK, lambda n, me_ref: (0, 0))],
            scratch_shapes=[pltpu.VMEM((features, tile), hold)],
        ),
        out_shape=[jax.ShapeDtypeStruct(o, HALF) for o in outs]
        + [jax.ShapeDtypeStruct(MARK, WIDE)],
        compiler_params=pltpu.CompilerParams(
            dimension_semantics=("arbitrary",), vmem_limit_bytes=VMEM_BYTES
        ),
        cost_estimate=cost(TAKES[name]),
        name=name,
    )(me, left, *rights, *after)
    return found


def split_kernel(plan, core_ref, *refs):
    ins, outs = refs[: len(plan)], list(refs[len(plan) :])
    for ref, (kind, groups, chips) in zip(ins, plan):
        if kind == "cast":
            outs.pop(0)[...] = ref[...].astype(HALF)
            continue
        size = ref.shape[1] // (groups * chips * 2)
        pick = lambda odd: jnp.concatenate(
            [ref[:, (2 * k + odd) * size : (2 * k + odd + 1) * size] for k in range(groups * chips)],
            axis=1,
        )
        even, odd = pick(0), pick(1)
        is_even = core_ref[0] == 0
        own = jnp.where(is_even, even, odd).astype(HALF)
        other = jnp.where(is_even, odd, even).astype(HALF)
        if kind == "split":
            outs.pop(0)[...] = own
            outs.pop(0)[...] = other
        else:
            out = outs.pop(0)
            out[:, : own.shape[1]] = own
            out[:, own.shape[1] :] = other


def split_call(name, core, weights, plan):
    outs = []
    for weight, (kind, _, _) in zip(weights, plan):
        size, columns = weight.shape
        if kind == "split":
            outs += [jax.ShapeDtypeStruct((size, columns // 2), HALF)] * 2
        else:
            outs.append(jax.ShapeDtypeStruct((size, columns), HALF))
    return pl.pallas_call(
        functools.partial(split_kernel, plan),
        in_specs=[pl.BlockSpec(memory_space=pltpu.SMEM)]
        + [pl.BlockSpec(memory_space=pltpu.VMEM)] * len(weights),
        out_specs=[pl.BlockSpec(memory_space=pltpu.VMEM)] * len(outs),
        out_shape=outs,
        compiler_params=pltpu.CompilerParams(vmem_limit_bytes=VMEM_BYTES),
        cost_estimate=cost(TAKES[name]),
        name=name,
    )(core, *weights)


def pack_kernel(width, split_count, chips, core_ref, *refs):
    *ins, out = refs
    at = 0
    for k in range(split_count):
        own, other = ins[2 * k], ins[2 * k + 1]
        rows = own.shape[0]
        is_even = core_ref[0] == 0
        for column in range(0, own.shape[1], width):
            mine, came = own[:, column : column + width], other[:, column : column + width]
            out[at : at + rows, :] = jnp.where(is_even, mine, came)
            out[at + rows : at + 2 * rows, :] = jnp.where(is_even, came, mine)
            at += 2 * rows
    for ref in ins[2 * split_count :]:
        rows, columns = ref.shape
        if chips and ref is ins[-1]:
            size = columns // (2 * chips)
            even, odd = (
                jnp.concatenate(
                    [ref[:, (2 * k + o) * size : (2 * k + o + 1) * size] for k in range(chips)],
                    axis=1,
                )
                for o in (0, 1)
            )
            is_even = core_ref[0] == 0
            whole = [jnp.where(is_even, even, odd), jnp.where(is_even, odd, even)]
            found = [v[:, c : c + width] for v in whole for c in range(0, columns // 2, width)]
        else:
            found = [ref[:, c : c + width] for c in range(0, columns, width)]
        for value in found:
            out[at : at + rows, :] = value.astype(HALF)
            at += rows


def pack_call(name, core, width, split, plain, chips=0):
    ins = [a for pair in split for a in pair] + list(plain)
    size = sum(a.size for a in ins) // width
    return pl.pallas_call(
        functools.partial(pack_kernel, width, len(split), chips),
        in_specs=[pl.BlockSpec(memory_space=pltpu.SMEM)]
        + [pl.BlockSpec(memory_space=pltpu.VMEM)] * len(ins),
        out_specs=pl.BlockSpec(memory_space=pltpu.VMEM),
        out_shape=jax.ShapeDtypeStruct((size, width), HALF),
        compiler_params=pltpu.CompilerParams(vmem_limit_bytes=VMEM_BYTES),
        cost_estimate=cost(TAKES[name]),
        name=name,
    )(core, *ins)


def condition_kernel(buckets, labels, times, classes, out, one, two, sems):
    count = out.shape[0]

    def copies(i):
        yield pltpu.make_async_copy(
            times.at[pl.ds(buckets[i], 1), :], one.at[pl.ds(i, 1), :], sems.at[0, i]
        )
        yield pltpu.make_async_copy(
            classes.at[pl.ds(labels[i], 1), :], two.at[pl.ds(i, 1), :], sems.at[1, i]
        )

    for i in range(count):
        for copy in copies(i):
            copy.start()
    for i in range(count):
        for copy in copies(i):
            copy.wait()
    out[...] = one[...] + two[...]


def condition_call(buckets, labels, times, classes):
    shape = (buckets.shape[0], times.shape[1])
    return pl.pallas_call(
        condition_kernel,
        in_specs=[pl.BlockSpec(memory_space=pltpu.SMEM)] * 2
        + [pl.BlockSpec(memory_space=pl.ANY)] * 2,
        out_specs=pl.BlockSpec(memory_space=pltpu.VMEM),
        out_shape=jax.ShapeDtypeStruct(shape, WIDE),
        scratch_shapes=[
            pltpu.VMEM(shape, WIDE),
            pltpu.VMEM(shape, WIDE),
            pltpu.SemaphoreType.DMA((2, shape[0])),
        ],
        cost_estimate=cost(TAKES["condition"]),
        name="condition",
    )(buckets, labels, times, classes)


def join_kernel(groups, chips, core_ref, own, other, out):
    size = own.shape[1] // (groups * chips)
    is_even = core_ref[0] == 0
    even = jnp.where(is_even, own[...], other[...]).astype(WIDE)
    odd = jnp.where(is_even, other[...], own[...]).astype(WIDE)
    parts = []
    for k in range(groups * chips):
        parts += [v[:, k * size : (k + 1) * size] for v in (even, odd)]
    out[...] = jnp.concatenate(parts, axis=1)


def join_call(name, core, own, other, groups, chips):
    rows, columns = own.shape
    return pl.pallas_call(
        functools.partial(join_kernel, groups, chips),
        in_specs=[pl.BlockSpec(memory_space=pltpu.SMEM)]
        + [pl.BlockSpec(memory_space=pltpu.VMEM)] * 2,
        out_specs=pl.BlockSpec(memory_space=pltpu.VMEM),
        out_shape=jax.ShapeDtypeStruct((rows, 2 * columns), WIDE),
        compiler_params=pltpu.CompilerParams(vmem_limit_bytes=VMEM_BYTES),
        cost_estimate=cost(4),
        name=name,
    )(core, own, other)


def last_kernel(value, *refs):
    refs[-1][...] = value[...]


def last_call(value, after):
    return pl.pallas_call(
        last_kernel,
        in_specs=[pl.BlockSpec(memory_space=pltpu.VMEM)]
        + [pl.BlockSpec(memory_space=pl.ANY)] * len(after),
        out_specs=pl.BlockSpec(memory_space=pltpu.VMEM),
        out_shape=jax.ShapeDtypeStruct(value.shape, value.dtype),
        cost_estimate=cost(1),
        name="last",
    )(value, *after)


def shards(
    n_dp,
    n_seq,
    image_tokens,
    cotangent,
    targets,
    bucket,
    labels,
    time_table,
    class_table,
    ada_weight,
    ada_bias,
    qkv_weight,
    qkv_bias,
    out_weight,
    out_bias,
    up_weight,
    up_bias,
    down_weight,
    down_bias,
    tap_first,
    tap_first_bias,
    tap_second,
    tap_second_bias,
    tap_third,
    tap_third_bias,
):
    images, part_rows, width = image_tokens.shape
    chips = n_dp // 2
    bits = chips.bit_length() - 1
    assert 1 << bits == chips and 2 * images == n_seq and n_seq & (n_seq - 1) == 0
    rows = 2 * images * part_rows
    place = lax.axis_index("dp")
    plane = lax.axis_index("seq")
    core, chip = place % 2, place // 2
    first_core = core == 0
    me = chip.astype(jnp.int32).reshape(1)

    def flip_core(array):
        return lax.ppermute(array, "dp", [(i, i ^ 1) for i in range(n_dp)])

    def flip_chip(array, bit):
        return lax.ppermute(array, "dp", [(i, i ^ (2 << bit)) for i in range(n_dp)])

    def flip_plane(array, bit):
        return lax.ppermute(array, "seq", [(i, i ^ (1 << bit)) for i in range(n_seq)])

    spent = []

    def later(array, *done):
        if not done:
            return array
        marks = []
        for item in done:
            item = DONE[item] if isinstance(item, str) else item
            marks.append(item)
        array, *marks = lax.optimization_barrier((array, *marks))
        spent.extend(marks)
        return array

    def pull(have, level, first):
        for r in range(chips):
            if r.bit_count() == level:
                bit = next(
                    b for b in ((first + k) % bits for k in range(bits)) if r >> b & 1
                )
                have[r] = flip_chip(have[r ^ 1 << bit], bit)

    def ranks(first):
        order = [(first + k) % bits for k in range(bits)]
        return sorted(range(chips), key=lambda r: [r >> b & 1 for b in order])

    def scatter_begin(arrays, plan, *done, under_way=()):
        found = []
        for k, (order, _, _) in enumerate(plan):
            first = next(f for f in range(bits) if ranks(f) == order)
            came = under_way[k] if under_way else flip_chip(arrays[2 * k + 1], first)
            found.append(([arrays[2 * k], later(came, *done)], first))
        sent = []
        for parts, first in found:
            for step in range(1, bits):
                half = parts[0].shape[0] // 2
                far = sum(p[half:].astype(WIDE) for p in parts).astype(HALF)
                came = flip_chip(far, (first + step) % bits)
                parts = [p[:half] for p in parts] + [came]
            sent.append(parts)
        return sent, [parts[1] for parts, _ in found]

    def scatter_end(sent, *done):
        found = [
            sum(p.astype(WIDE) for p in (*parts[:-1], later(parts[-1], *done))).astype(HALF)
            for parts in sent
        ]
        return found[0] if len(found) == 1 else jnp.concatenate(found)

    def halves(size):
        if size % 32:
            return [(ranks(0), 0, size)]
        return [(ranks(0), 0, size // 2), (ranks(1 % bits), size // 2, size // 2)]

    def sum_line(array, *windows):
        extra = n_seq // 4
        for bit in range(extra.bit_length() - 1):
            array = (array.astype(WIDE) + flip_plane(array, bit).astype(WIDE)).astype(HALF)

        def move(what, pairs):
            pairs = [(a * extra + k, b * extra + k) for a, b in pairs for k in range(extra)]
            return lax.ppermute(what, "seq", pairs)

        at = plane // extra
        half = array.shape[0] // 2
        came = later(move(array, [(0, 1), (3, 2)]), *windows)
        array = (array.astype(WIDE) + came.astype(WIDE)).astype(HALF)
        low, high = array[:half], array[half:]
        came = move(jnp.where(at == 1, high, low), [(1, 2), (2, 1)])
        kept = (jnp.where(at == 1, low, high).astype(WIDE) + came.astype(WIDE)).astype(HALF)
        came = move(kept, [(1, 2), (2, 1)])
        array = jnp.where(
            at == 1, jnp.concatenate([kept, came]), jnp.concatenate([came, kept])
        )
        came = move(array, [(1, 0), (2, 3)])
        return jnp.where((at == 1) | (at == 2), array, came)

    def sum_planes(array, seen=None, half_way=None):
        steps = range(n_seq.bit_length() - 1)
        for bit in steps:
            half = array.shape[0] // 2
            low, high = array[:half], array[half:]
            upper = (plane >> bit & 1) == 1
            came = flip_plane(jnp.where(upper, low, high), bit)
            if seen is not None:
                seen.append(came)
            array = (jnp.where(upper, high, low).astype(WIDE) + came.astype(WIDE)).astype(HALF)
        for bit in reversed(steps):
            if half_way is not None and bit == 0:
                array = later(array, half_way)
            came = flip_plane(array, bit)
            if seen is not None:
                seen.append(came)
            upper = (plane >> bit & 1) == 1
            array = jnp.where(
                upper, jnp.concatenate([came, array]), jnp.concatenate([array, came])
            )
        return array

    def routes(turn):
        pairs = []
        for at in range(n_dp):
            for z in range(n_seq):
                k = z ^ turn
                goal = (at - at % 2 + k // images, (at % 2) * images + k % images)
                pairs.append((at * n_seq + z, goal[0] * n_seq + goal[1]))
        return pairs

    def to_chip(array, depth, *after):
        half = array.shape[1] // 2
        found = []
        for turn in range(n_seq):
            k = plane ^ turn
            piece = lax.dynamic_slice(
                array, (k % images, (k // images) * half, 0), (1, half, array.shape[2])
            )[0]
            piece = later(piece, *([found[-depth]] if len(found) >= depth else []), *after)
            found.append(lax.ppermute(piece, ("dp", "seq"), routes(turn)))
        return found

    def from_chip(array, depth, windows=((),) * 4):
        half = array.shape[0] // n_seq
        found = []
        for turn in range(n_seq):
            back = [(b, a) for a, b in routes(turn)]
            piece = array[turn * half : (turn + 1) * half]
            piece = later(piece, *([found[-depth]] if len(found) >= depth else []))
            came = lax.ppermute(piece, ("dp", "seq"), back)
            found.append(later(came, *windows[turn % len(windows)]))
        pieces = list(found)
        stacked = jnp.stack(found)
        for bit in range(n_seq.bit_length() - 1):
            pairs = stacked.reshape(-1, 2, 1 << bit, *stacked.shape[1:])
            swapped = jnp.where((plane >> bit & 1) == 1, pairs[:, ::-1], pairs)
            stacked = swapped.reshape(stacked.shape)
        parts = stacked.reshape(2, images, half, array.shape[1])
        return parts.transpose(1, 0, 2, 3).reshape(images, 2 * half, array.shape[1]), pieces

    def by_core(array, groups):
        lead = array.shape[:-1]
        cut = array.reshape(*lead, groups, chips, 2, -1)
        even = cut[..., 0, :].reshape(*lead, -1)
        odd = cut[..., 1, :].reshape(*lead, -1)
        return jnp.where(first_core, even, odd), jnp.where(first_core, odd, even)

    def from_cores(own, other, groups):
        lead = own.shape[:-1]
        even = jnp.where(first_core, own, other).reshape(*lead, groups, chips, 1, -1)
        odd = jnp.where(first_core, other, own).reshape(*lead, groups, chips, 1, -1)
        return jnp.concatenate([even, odd], axis=-2).reshape(*lead, -1)

    def in_order(own, other):
        return jnp.where(
            first_core, jnp.concatenate([own, other]), jnp.concatenate([other, own])
        )

    def spread(array, columns):
        return jnp.concatenate(
            [array[:, k : k + columns] for k in range(0, array.shape[1], columns)]
        )

    def weight_of(groups, columns, height):
        if all(v % 16 == 0 for _, pieces in groups for p in pieces for v in (p[0], p[1], p[4], height)):
            arrays, found = [], []
            for places, pieces in groups:
                numbers = []
                for array, base in places:
                    known = [k for k, seen in enumerate(arrays) if seen is array]
                    numbers.append((known[0] if known else len(arrays), base))
                    if not known:
                        arrays.append(array)
                found.append((numbers, pieces))
            return arrays, (found, True, height, columns)
        blocks = []
        for r in range(chips):
            block = jnp.zeros((height, columns), HALF)
            for places, pieces in groups:
                array, base = places[r]
                for row, rows, column, wide, to_row, to_column in pieces:
                    part = array[base + row : base + row + rows, column : column + wide]
                    block = lax.dynamic_update_slice(block, part, (to_row, to_column))
            blocks.append(block)
        stacked = jnp.take(jnp.stack(blocks), jnp.arange(chips) ^ chip, axis=0)
        stacked = stacked.reshape(-1, columns)
        size = stacked.shape[0]
        return [stacked], ([([(0, 0)], [(0, size, 0, columns, 0, 0)])], False, size, columns)

    def stacked_weight(places, at, width, columns, height):
        pieces = [
            (at + k * height, height, 0, width, 0, k * width) for k in range(columns // width)
        ]
        return weight_of([(places, pieces)], columns, height)

    biases = (
        ada_bias,
        qkv_bias,
        out_bias,
        up_bias,
        down_bias,
        tap_first_bias,
        tap_second_bias,
        tap_third_bias,
    )
    core_at = core.astype(jnp.int32).reshape(1)
    qkv_own, qkv_other = split_call("split_qkv", core_at, [qkv_weight], [("split", 3, chips)])
    qkv_have = {0: in_order(qkv_own, flip_core(qkv_other))}
    pull(qkv_have, 1, 0)
    qkv_near = [qkv_have[1 << b] for b in range(bits)]
    def pull_rest(have, first):
        for level in range(2, bits + 1):
            pull(have, level, first)
        return [have[r] for r in range(chips) if r.bit_count() > 1]

    def pull_parts(have, split):
        places, came = [[None] * chips for _ in range(2)], []
        for k in range(2):
            part = {r: have[r][:split] if k == 0 else have[r][split:] for r in have}
            came.append(pull_rest(part, 1 - k))
            for r in range(chips):
                places[k][r] = (have[r], k * split) if r in have else (part[r], 0)
        return places, came

    qkv_height, qkv_columns = qkv_have[0].shape
    (low_places, high_places), (low_last, high_last) = pull_parts(qkv_have, qkv_height // 2)
    qkv_weights = weight_of(
        [
            (places, [(0, qkv_height // 2, 0, qkv_columns, at, 0)])
            for places, at in ((low_places, 0), (high_places, qkv_height // 2))
        ],
        qkv_columns,
        qkv_height,
    )
    qkv_rest = low_last + high_last
    packed = jnp.concatenate(biases).astype(HALF).astype(WIDE)
    packed = jnp.concatenate([packed, jnp.concatenate([bucket, labels]).astype(WIDE)])
    everyone = jnp.pad(packed, (0, -packed.shape[0] % 128)).reshape(1, -1)
    everyone = jnp.concatenate([everyone, flip_core(everyone)])
    for bit in range(bits):
        everyone = jnp.concatenate([everyone, flip_chip(everyone, bit)])
    everyone = jnp.concatenate(
        [
            lax.dynamic_slice(everyone, (place ^ d, 0), (1, everyone.shape[1]))
            for d in range(n_dp)
        ]
    )
    full, at = [], 0
    for bias in biases:
        full.append(everyone[:, at : at + bias.shape[0]].reshape(1, -1))
        at += bias.shape[0]
    bucket_all = everyone[:, at : at + images].reshape(-1).astype(jnp.int32)
    labels_all = everyone[:, at + images : at + 2 * images].reshape(-1).astype(jnp.int32)
    ada_bias_full, qkv_bias_full, out_bias_full, up_bias_full = full[:4]
    down_bias_full, first_bias_full, second_bias_full, third_bias_full = full[4:]
    qkv_bias_own = by_core(qkv_bias_full, 3)[0]
    up_bias_own = by_core(up_bias_full, 1)[0]
    first_bias_own = by_core(first_bias_full, 1)[0]
    second_bias_own = by_core(second_bias_full, 1)[0]

    up_weight = later(up_weight, qkv_have[0])
    up_own, up_other, first_own, first_other = split_call(
        "split_rest",
        core_at,
        [up_weight, tap_first],
        [("split", 1, chips), ("split", 1, chips)],
    )
    up_came, first_came = flip_core(up_other), flip_core(first_other)
    wide, narrow = width, math.gcd(tap_second.shape[1], tap_third.shape[1])
    near = pack_call(
        "pack_near", core_at, wide, [(up_own, up_came)], [down_weight, out_weight]
    )
    condition = condition_call(later(bucket_all, near, *qkv_near), labels_all, time_table, class_table)
    shard = ada_weight.shape[0]
    condition_own = lax.dynamic_slice(
        condition, (0, place * shard), (condition.shape[0], shard)
    )
    cond_act, cond_back = jax.vjp(jax.nn.silu, condition_own)
    cond_low = cond_act.astype(HALF)
    cond_plane = lax.dynamic_index_in_dim(
        cond_low.reshape(chips, n_seq, shard), plane, axis=1, keepdims=False
    )
    ada_low = ada_weight.astype(HALF)
    modulation = jnp.dot(cond_plane, ada_low, preferred_element_type=WIDE)
    modulation = later(modulation, *qkv_rest)
    modulation = modulation + flip_core(modulation)
    ranked = [
        lax.dynamic_slice(modulation, (chip ^ r, 0), (1, modulation.shape[1]))
        for r in range(chips)
    ]
    for bit in reversed(range(bits)):
        half = 1 << bit
        came = flip_chip(jnp.concatenate(ranked[half : 2 * half]), bit)
        ranked = [ranked[r] + came[r : r + 1] for r in range(half)]
    modulation = ranked[0] + ada_bias_full
    shift_one, scale_one, gate_one, shift_two, scale_two, gate_two = jnp.split(
        modulation, 6, axis=-1
    )

    same_core = [[2 * k + c for k in range(chips)] for c in range(2)]


    far = pack_call(
        "pack_far",
        core_at,
        narrow,
        [(first_own, first_came)],
        [tap_third, later(tap_second, qkv_have[1])],
        chips,
    )
    tokens_pieces = to_chip(image_tokens, 1)
    tokens_own = jnp.concatenate(tokens_pieces, axis=0)
    near_have = {0: later(near, modulation, *qkv_rest)}
    pull(near_have, 1, 0)
    near_own = [near_have[1 << b] for b in range(bits)]

    tile = 256 if rows % 512 == 0 else rows // 2
    heads = HEADS // 2
    tokens = jnp.concatenate([tokens_own, flip_core(tokens_own)])
    head_shape = (heads, rows, HEAD_DIM)
    inner = heads * HEAD_DIM
    hidden_ff = up_weight.shape[1] // 2
    tap_width = tap_first.shape[1] // 2
    tap_out = tap_third.shape[1]

    def flat(columns, dtype):
        return ((rows, columns), dtype, 0)

    def turned(columns):
        return ((columns, rows), HALF, 1)

    call = functools.partial(token_call, rows=rows, tile=tile)
    twice = functools.partial(token_call, rows=rows, tile=2 * tile)
    hidden_one_t, query, key, value = call(
        "qkv",
        qkv_body,
        me,
        [(tokens, False)],
        [shift_one, scale_one, qkv_bias_own],
        [qkv_weights],
        [turned(width)] + [(head_shape, HALF, 1)] * 3,
        [],
    )
    context, lse = attention_call(query, key, value)
    for r in [r for r in near_have if r]:
        near_have[r] = later(near_have[r], "attention")
    far_have = {0: far}
    height, high = 2 * up_own.shape[0], tap_second.shape[0]
    columns, tap_columns = up_own.shape[1], first_own.shape[1]
    cut = height * columns // wide
    (up_places, mixed_places), (up_last, _) = pull_parts(near_have, cut)
    up_weights = stacked_weight(up_places, 0, wide, columns, height)
    down_weights = stacked_weight(mixed_places, 0, wide, wide, down_weight.shape[0])
    out_weights = stacked_weight(
        mixed_places, down_weight.shape[0], wide, wide, out_weight.shape[0]
    )
    for bit in range(bits):
        far_have[1 << bit] = flip_chip(later(far, *near_own), bit)
    cut = height * tap_columns // narrow + high * tap_third.shape[1] // narrow
    (first_places, second_places), _ = pull_parts(far_have, cut)
    first_weights = stacked_weight(first_places, 0, narrow, tap_columns, height)
    third_weights = stacked_weight(
        first_places, height * tap_columns // narrow, narrow, tap_third.shape[1], high
    )
    second_weights = stacked_weight(second_places, 0, narrow, tap_second.shape[1], high)

    beside_pieces = to_chip(
        later(jnp.concatenate([cotangent, targets], axis=2), "qkv"), 1
    )
    beside = jnp.concatenate(beside_pieces)
    out_part, out_low, context_t = call(
        "out",
        out_body,
        me,
        [(context, False)],
        [],
        [out_weights],
        [flat(width, WIDE), flat(width, HALF), turned(inner)],
        [],
        after=[*up_last, far, beside_pieces[1]],
    )
    out_came = flip_core(out_low)
    mixed, hidden_two_t, upper, act_t, feed_part, feed_low = call(
        "feed",
        feed_body,
        me,
        [(tokens, False), (out_part, False), (out_came, True)],
        [gate_one, shift_two, scale_two, out_bias_full, up_bias_own],
        [up_weights, down_weights],
        [
            flat(width, WIDE),
            turned(width),
            flat(hidden_ff, WIDE),
            turned(hidden_ff),
            flat(width, WIDE),
            flat(width, HALF),
        ],
        [],
        after=[beside, *[far_have[1 << b] for b in range(bits)]],
    )
    feed_came = flip_core(feed_low)
    beside_all = jnp.concatenate([beside, flip_core(beside)])
    cotangent_all, targets_all = beside_all[:, :width], beside_all[:, width:]
    block_out, block_t, first_pre, first_t, second_part, second_low = call(
        "tap",
        tap_body,
        me,
        [(mixed, False), (feed_part, False), (feed_came, True)],
        [gate_two, down_bias_full, first_bias_own],
        [first_weights, second_weights],
        [
            flat(width, HALF),
            turned(width),
            flat(tap_width, WIDE),
            turned(tap_width),
            flat(tap_width, WIDE),
            flat(tap_width, HALF),
        ],
        [],
    )
    second_came = flip_core(second_low)
    second_pre, second_t, latent_part, latent_low = call(
        "latent",
        latent_body,
        me,
        [(second_part, False), (second_came, True)],
        [second_bias_own],
        [third_weights],
        [flat(tap_width, WIDE), turned(tap_width), flat(tap_out, WIDE), flat(tap_out, HALF)],
        [],
    )
    latent_came = flip_core(latent_low)

    dlatent, dsecond, cos_sum, third_bg, second_bg = call(
        "cosine",
        cosine_body,
        me,
        [(latent_part, False), (latent_came, True), (targets_all, False), (second_pre, False)],
        [third_bias_full],
        [third_weights],
        [flat(tap_out, HALF), flat(tap_width, HALF)],
        [(1, 128), (1, tap_out), (1, tap_width)],
    )
    dsecond_came = flip_core(dsecond)
    third_plan = [(ranks(1 % bits), 0, tap_third.shape[0])]
    third_wg = weight_grad_call("third_grad", me, second_t, [dlatent], third_plan, 384)
    second_plan = halves(tap_second.shape[0])
    second_wg = weight_grad_call(
        "second_grad", me, first_t, [dsecond, dsecond_came], second_plan, 512, after=third_wg[:1]
    )
    dfirst, tap_part, tap_low, first_bg = call(
        "tap_back",
        tap_back_body,
        me,
        [(dsecond, False), (dsecond_came, True), (first_pre, False)],
        [],
        [second_weights, first_weights],
        [flat(tap_width, HALF), flat(width, WIDE), flat(width, HALF)],
        [(1, tap_width)],
        after=[second_wg[0]],
    )
    tap_came = flip_core(tap_low)
    block_output, block_pieces = from_chip(
        block_out[: rows // 2], 2, (("cosine",), ("cosine",), ("tap_back",), ("tap_back",))
    )
    third_sent, third_far = scatter_begin(third_wg, third_plan, "tap_back")
    first_plan = [(ranks(1 % bits), 0, height)]
    first_wg = weight_grad_call(
        "first_grad", me, block_t, [dfirst], first_plan, 512, after=third_far + block_pieces[:2]
    )
    doutput, dfeed, dupper, hidden_part, hidden_low, gate_two_grad, down_bg, up_bg = call(
        "feed_back",
        feed_back_body,
        me,
        [
            (cotangent_all, False),
            (tap_part, False),
            (tap_came, True),
            (feed_part, False),
            (feed_came, True),
            (upper, False),
        ],
        [gate_two, down_bias_full],
        [down_weights, up_weights],
        [
            flat(width, WIDE),
            flat(width, HALF),
            flat(hidden_ff, HALF),
            flat(width, WIDE),
            flat(width, HALF),
        ],
        [(1, width), (1, width), (1, hidden_ff)],
        after=[first_wg[0], *block_pieces],
    )

    first_sent, first_far = scatter_begin(first_wg, first_plan, "feed_back")
    third_part = lax.psum(scatter_end(third_sent, "first_grad"), "seq")
    hidden_came = flip_core(hidden_low)
    down_plan = halves(down_weight.shape[0])
    down_wg = weight_grad_call(
        "down_grad", me, act_t, [dfeed], down_plan, 256, after=[*first_far, third_part]
    )
    second_sent, second_far = scatter_begin(second_wg, second_plan, "down_grad")
    up_plan = halves(height)
    up_wg = weight_grad_call(
        "up_grad", me, hidden_two_t, [dupper], up_plan, 768, after=[down_wg[0], *second_far]
    )
    first_sum = scatter_end(first_sent, "down_grad")
    first_sum = lax.psum(later(first_sum, third_part), "seq")
    (
        dmixed,
        dattended,
        dcontext,
        shift_two_grad,
        scale_two_grad,
        gate_one_grad,
        out_bg,
    ) = call(
        "mix_back",
        mix_back_body,
        me,
        [
            (mixed, False),
            (doutput, False),
            (hidden_part, False),
            (hidden_came, True),
            (out_part, False),
            (out_came, True),
        ],
        [scale_two, gate_one, out_bias_full],
        [out_weights],
        [flat(width, WIDE), flat(width, HALF), (head_shape, HALF, 1)],
        [(1, width)] * 4,
        after=[up_wg[0]],
    )
    down_sent, down_far = scatter_begin(down_wg, down_plan, "mix_back")
    out_plan = [(ranks(0), 0, out_weight.shape[0])]
    out_wg = weight_grad_call(
        "out_grad", me, context_t, [dattended], out_plan, 384
    )
    dquery, dkey, dvalue = attention_back_call(
        query, key, value, dcontext, lse, after=[out_wg[0], first_sum, *[parts[-1] for parts in down_sent]]
    )
    second_sum = scatter_end(second_sent, "mix_back")
    second_sum = lax.psum(later(second_sum, first_sum), "seq")
    up_under_way = [
        flip_chip(later(up_wg[2 * k + 1], *down_far), k) for k in range(len(up_plan))
    ]
    up_sent, up_far = scatter_begin(
        up_wg, up_plan, "attention_back", under_way=up_under_way
    )
    dqkv, one_part, one_low, qkv_bg = call(
        "qkv_back",
        qkv_back_body,
        me,
        [(dquery, False), (dkey, False), (dvalue, False)],
        [],
        [qkv_weights],
        [flat(3 * inner, HALF), flat(width, WIDE), flat(width, HALF)],
        [(1, 3 * inner)],
        after=[second_sum, *up_far],
    )
    one_came = flip_core(one_low[rows // 2 :])
    qkv_plan = halves(qkv_have[0].shape[0])
    out_sent, out_far = scatter_begin(out_wg, out_plan, "qkv_back")
    qkv_wg = weight_grad_call(
        "qkv_grad", me, hidden_one_t, [dqkv], qkv_plan, 256
    )
    up_part = scatter_end(up_sent, "qkv_grad")
    out_part = scatter_end(out_sent, "qkv_grad")
    down_part = scatter_end(down_sent, "attention_back")
    down_part = lax.psum(later(down_part, second_sum), "seq")
    up_part = lax.psum(later(up_part, down_part), "seq")
    input_low, shift_one_grad, scale_one_grad = token_call(
        "input_grad",
        input_body,
        me,
        [(tokens, False), (dmixed, False), (one_part, False), (one_came, False)],
        [scale_one],
        [],
        [((rows // 2, width), HALF, 0)],
        [(1, width)] * 2,
        rows=rows // 2,
        tile=tile,
        after=[qkv_wg[0], down_part, *out_far],
    )
    input_grad = from_chip(input_low, 2)[0].astype(WIDE)

    qkv_sent, qkv_far = scatter_begin(qkv_wg, qkv_plan, "input_grad")
    qkv_scattered = scatter_end(qkv_sent)
    qkv_part, out_part = lax.psum((later(qkv_scattered, up_part), out_part), "seq")
    qkv_hops = [qkv_scattered, qkv_scattered]
    one_grads = jnp.concatenate([shift_one_grad, scale_one_grad], axis=1)
    one_grads = later(one_grads + flip_core(one_grads), *qkv_far)
    modulation_grad = jnp.concatenate(
        [one_grads, gate_one_grad, shift_two_grad, scale_two_grad, gate_two_grad], axis=1
    )
    for bit in range(bits):
        modulation_grad = jnp.concatenate([modulation_grad, flip_chip(modulation_grad, bit)])
    modulation_grad = later(modulation_grad, up_part)
    for bit in range(n_seq.bit_length() - 1):
        modulation_grad = jnp.concatenate([modulation_grad, flip_plane(modulation_grad, bit)])
    nth = jnp.arange(chips * n_seq)
    picked = ((nth % chips) ^ chip) * n_seq + ((nth // chips) ^ plane)
    pick = (picked[:, None] == jnp.arange(chips * n_seq)[None, :]).astype(WIDE)
    modulation_all = later(jnp.dot(pick.T, modulation_grad, precision=HIGH), qkv_hops[-1])
    ada_wg = jnp.einsum(
        "bi,bj->ij", cond_low.astype(WIDE), modulation_all, precision=HIGH
    )
    ada_size = ada_bias.shape[0]
    ada_bg = lax.dynamic_slice(jnp.sum(modulation_all, axis=0), (place * ada_size,), (ada_size,))
    cond_grad = cond_back(
        jnp.einsum("bj,ij->bi", modulation_all, ada_low.astype(WIDE), precision=HIGH)
    )[0]
    cond_grad = lax.all_gather(cond_grad, "dp", axis=1, tiled=True)
    time_hot = (
        bucket_all[:, None] == jnp.arange(time_table.shape[0], dtype=jnp.int32)[None, :]
    ).astype(WIDE)
    class_hot = (
        labels_all[:, None] == jnp.arange(class_table.shape[0], dtype=jnp.int32)[None, :]
    ).astype(WIDE)
    time_grad = jnp.einsum("bt,bd->td", time_hot, cond_grad, precision=HIGH)
    class_grad = jnp.einsum("bt,bd->td", class_hot, cond_grad, precision=HIGH)

    sums = [qkv_bg, up_bg, first_bg, second_bg, out_bg, down_bg, third_bg, cos_sum]
    line = later(jnp.concatenate(sums, axis=1), qkv_scattered)
    for bit in range(bits):
        line = line + flip_chip(line, bit)
    for bit in range(n_seq.bit_length() - 1):
        line = line + flip_plane(line, bit)
    line = later(line, qkv_hops[0])
    split_at = sum(s.shape[1] for s in sums[:4])
    came = flip_core(line[:, :split_at])
    bias_grads, at = [], 0
    for k, (item, groups) in enumerate(zip(sums[:4], (3, 1, 1, 1))):
        size = item.shape[1]
        bias_grads.append(
            from_cores(line[:, at : at + size], came[:, at : at + size], groups)
        )
        at += size
    for item in sums[4:7]:
        bias_grads.append(line[:, at : at + item.shape[1]])
        at += item.shape[1]
    align_loss = -0.5 * line[:, at : at + 1] / (rows * chips * n_seq)

    def own_part(grad):
        size = grad.shape[1] // n_dp
        return lax.dynamic_slice(grad, (0, place * size), (1, size))[0]

    qkv_bo, up_bo, first_bo, second_bo, out_bo, down_bo, third_bo = map(own_part, bias_grads)

    def whole_columns(grad, groups):
        size = grad.shape[0] // 2
        own = lax.dynamic_slice(grad, (core * size, 0), (size, grad.shape[1]))
        other = lax.dynamic_slice(grad, ((1 - core) * size, 0), (size, grad.shape[1]))
        return join_call("join", core_at, own, flip_core(other), groups, chips)

    block_output = later(block_output, "input_grad")
    third_part, second_sum, first_sum, down_part, up_part, out_part = (
        later(a, "input_grad", qkv_scattered)
        for a in (third_part, second_sum, first_sum, down_part, up_part, out_part)
    )
    third_own = third_part.astype(WIDE)
    second_own = join_call(
        "join", core_at, second_sum[:, :tap_width], second_sum[:, tap_width:], 1, chips
    )
    first_own = whole_columns(first_sum, 1)
    down_own = down_part.astype(WIDE)
    up_own = whole_columns(up_part, 1)
    out_own = out_part.astype(WIDE)
    qkv_own = whole_columns(qkv_part, 3)
    align_loss = last_call(align_loss, spent)[0, 0]
    return (
        block_output,
        input_grad,
        align_loss,
        time_grad,
        class_grad,
        ada_wg,
        ada_bg,
        qkv_own,
        qkv_bo,
        out_own,
        out_bo,
        up_own,
        up_bo,
        down_own,
        down_bo,
        first_own,
        first_bo,
        second_own,
        second_bo,
        third_own,
        third_bo,
    )


def solution(mesh):
    tokens, rows, line = P("dp", "seq", None), P("dp", None), P("dp")
    return jax.shard_map(
        functools.partial(shards, mesh.shape["dp"], mesh.shape["seq"]),
        mesh=mesh,
        in_specs=(tokens, tokens, tokens, line, line, P(), P()) + (rows, line) * 8,
        out_specs=(tokens, tokens, P(), P(), P()) + (rows, line) * 8,
        check_vma=False,
    )
```
